256 devices in a mesh: dp: 32 (over z, y_hi, core), ctx: 8 (over x, y_lo).
Axes of the slice: x: 4, y: 4 (y_hi: 2, y_lo: 2; y = y_hi * 2 + y_lo), z: 8, core: 2. Of those that a mesh axis runs over, the one named last changes fastest.
Arguments:
- q_heads: bfloat16 [32, 1536, 2048], P('dp', 'ctx'), may hold values from -8 to 8
- keys: bfloat16 [32, 1536, 128], P('dp', 'ctx'), may hold values from -8 to 8
- values: bfloat16 [32, 1536, 128], P('dp', 'ctx'), may hold values from -6 to 6
- out_grad: bfloat16 [32, 1536, 2048], P('dp', 'ctx'), may hold values from -0.29882812 to 0.29882812
- hidden_in: bfloat16 [32, 1536, 16384], P('dp', 'ctx'), may hold values from -6 to 6
- doc_lengths: int32 [32, 8], P('dp'), may hold values from 1 to 576, 1536 in all within a row
- span_order: int32 [16], replicated, may hold values from 0 to 15, each once
- m_codes: int32 [16384, 256], P('dp'), may hold values from -127 to 127
- m_scales: float32 [2048], P('dp'), may hold values from 0.05 to 0.5
- v_codes: int32 [16384, 256], P('dp'), may hold values from 1 to 255
- v_scales: float32 [2048], P('dp'), may hold values from 0.05 to 1
Outputs:
- dq: bfloat16 [32, 1536, 2048], P('dp', 'ctx')
- update: float32 [16384, 256], P('dp')
- m_norm: float32 [16384, 256], P('dp')
- m_absmax: float32 [2048], P('dp')
- v_norm: float32 [16384, 256], P('dp')
- v_absmax: float32 [2048], P('dp')
The draws below stay inside these ranges and needn't reach their ends.
Inputs may be any that keep to these rules, and one draw needn't show every extreme that they name: `doc_lengths`: each sequence's 8 lengths sum to 1536. `span_order`: each stored block names a different position block.
All inputs are finite; a program needn't handle non-finite values. Where the reference program divides by a largest or mean magnitude, that divisor is 1e-20 or more.
Results may differ from the reference program's by a relative error of at most 0.0078.
Values may be sent and summed in bfloat16 or wider, within the bound.
A program may use at most 128 MiB of HBM per device.

```python
import math
import jax
import jax.numpy as jnp
import numpy as np
from jax import lax

D = 16384
HD = 128
HEADS = 16
TOK_DEV = 192
DOCS = 8
BLOCK = 2048
STEP = 10
SEQ_LEN = 1536
NBLK = 2048
N_DP = 32
N_CTX = 8


def draw_q_heads(key, part):
    shape = (N_DP, SEQ_LEN, HEADS * HD)
    own_key = jax.random.fold_in(key, 1)
    base = jnp.clip(jax.random.normal(own_key, shape, jnp.float32), -6.0, 6.0)
    return base.astype(jnp.bfloat16)


def draw_keys(key, part):
    shape = (N_DP, SEQ_LEN, HD)
    own_key = jax.random.fold_in(key, 2)
    base = jnp.clip(jax.random.normal(own_key, shape, jnp.float32), -6.0, 6.0)
    return base.astype(jnp.bfloat16)


def plant(entries, stream_key, least, high):
    place = [jax.random.randint(jax.random.fold_in(stream_key, axis), (), 0, length) for axis, length in enumerate(entries.shape)]
    main_axis = entries.shape.index(max(entries.shape))
    neighbour = place[:main_axis] + [(place[main_axis] + 1) % entries.shape[main_axis]] + place[main_axis + 1:]
    return entries.at[tuple(place)].set(least).at[tuple(neighbour)].set(high)


def strengthened(entries, stream_key, source, target, shards_of, factor):
    owner, partner = [(jnp.arange(entries.shape[axis_at]) // (entries.shape[axis_at] // shards_of)).reshape([-1 if axis == axis_at else 1 for axis in range(entries.ndim)]) for axis_at in (source, target)]
    chosen = jax.random.permutation(stream_key, shards_of)[partner]
    strong = (owner == chosen) | (owner == (partner + shards_of // 2) % shards_of)
    return jnp.where(strong, factor * entries, entries)


def steps_of(key, dims, pieces, least, largest):
    gain, own = 1.0, jax.random.fold_in(key, 6)
    for axis_at, shards_of in pieces:
        heights = jnp.exp(jax.random.uniform(jax.random.fold_in(own, axis_at), (shards_of,), jnp.float32, least / len(pieces), largest / len(pieces)))
        gain = gain * jnp.repeat(heights, dims[axis_at] // shards_of).reshape([-1 if axis == axis_at else 1 for axis in range(len(dims))])
    return gain


def profile(amount, total, most, lean):
    loads = [(1 << 20) // math.isqrt(rank ** lean) + 1 for rank in range(2, amount + 1)]
    spare, given = total - most - (amount - 1), [1] * (amount - 1)
    while spare > 0:
        free = [i for i in range(amount - 1) if given[i] < most]
        pool, left = sum([loads[i] for i in free]), spare
        for i in free:
            more = min(most - given[i], max(1, left * loads[i] // pool), spare)
            given[i] = given[i] + more
            spare = spare - more
    return np.array([most] + given)


def ragged_sizes(rng, amount, total, most, lean):
    if amount == 2:
        one = jax.random.randint(rng, (), max(1, total - most), min(most, total - 1) + 1)
        return jnp.stack([one, total - one])
    sizes = jnp.asarray(profile(amount, total, most, lean), jnp.int32)
    twos = (amount - 1) // 2
    source_of, taker = sizes[1:1 + 2 * twos:2], sizes[2:2 + 2 * twos:2]
    slack = jnp.minimum(source_of - 1, most - taker)
    moved = jax.random.randint(jax.random.fold_in(rng, 1), (twos,), 0, 1 << 20) % (slack + 1)
    sizes = sizes.at[1:1 + 2 * twos:2].set(source_of - moved).at[2:2 + 2 * twos:2].set(taker + moved)
    return sizes[jax.random.permutation(jax.random.fold_in(rng, 2), amount)]


def bell_draw(stream_key, shape, scale, bound, shards=(), held_as=jnp.bfloat16):
    loudness = steps_of(stream_key, shape, shards, -0.22, 0.18) if shards else 1.0
    entries = jax.random.normal(stream_key, shape, jnp.float32) * scale * loudness
    return jnp.minimum(jnp.maximum(entries, -bound), bound).astype(held_as)


def bell_draw_with(key, shape, scale, most, cuts, heavy, held_as=jnp.bfloat16):
    values = scale * jax.random.normal(key, shape, jnp.float32)
    if cuts:
        values = values * steps_of(key, shape, cuts, -0.22, 0.18)
    return jnp.clip(strengthened(values, jax.random.fold_in(key, 3), *heavy), -most, most).astype(held_as)


def setup_inputs(seed: int = 0) -> dict:
    seeds = jax.random.split(jax.random.key(seed), 12)
    q_heads = draw_q_heads(jax.random.fold_in(seeds[11], 71), 0)
    keys = draw_keys(jax.random.fold_in(seeds[11], 71), 0)
    values = bell_draw(seeds[2], (N_DP, SEQ_LEN, HD), 1.0, 6.0, ((0, 32), (1, 8)))
    out_grad = bell_draw(seeds[3], (N_DP, SEQ_LEN, HEADS * HD), 0.05, 0.29882812, ((0, 32), (1, 8)))
    hidden_in = bell_draw_with(seeds[4], (N_DP, SEQ_LEN, D), 1.0, 6.0, ((0, 32), (1, 8)), (0, 2, 32, 2.75))
    doc_lengths = jax.vmap(lambda own: ragged_sizes(own, DOCS, SEQ_LEN, 3 * SEQ_LEN // DOCS, 2))(jax.random.split(seeds[5], N_DP)).reshape((N_DP, DOCS)).astype(jnp.int32)
    span_order = jax.random.permutation(seeds[6], 2 * N_CTX).astype(jnp.int32)
    m_codes = plant(jax.random.randint(seeds[7], (D, 2 * HD), -127, 128), jax.random.fold_in(seeds[7], 1), -127, 127).astype(jnp.int32)
    m_scales = jnp.clip(jnp.exp(math.log(0.5) - 2.3025851 * jax.random.uniform(seeds[8], (NBLK,), jnp.float32) ** steps_of(seeds[8], (NBLK,), ((0, 32),), -0.2, 0.2)), 0.05, 0.5)
    v_codes = plant(jax.random.randint(seeds[9], (D, 2 * HD), 1, 256), jax.random.fold_in(seeds[9], 1), 1, 255).astype(jnp.int32)
    v_scales = jnp.clip(jnp.exp(math.log(1.0) - 2.9957323 * jax.random.uniform(seeds[10], (NBLK,), jnp.float32) ** steps_of(seeds[10], (NBLK,), ((0, 32),), -0.2, 0.2)), 0.05, 1.0)
    return dict(q_heads=q_heads, keys=keys, values=values, out_grad=out_grad, hidden_in=hidden_in, doc_lengths=doc_lengths, span_order=span_order, m_codes=m_codes, m_scales=m_scales, v_codes=v_codes, v_scales=v_scales)


def positions(order, span, total):
    rows = jnp.arange(total, dtype=jnp.int32)
    slot = rows // span
    match = slot[:, None] == jnp.arange(order.shape[0], dtype=jnp.int32)[None, :]
    first = lax.optimization_barrier(jnp.sum(jnp.where(match, order[None, :], 0), axis=1)).astype(jnp.int32)
    return first * span + rows % span

def documents(pos, lengths):
    ends = jnp.cumsum(lengths).astype(jnp.int32)
    return lax.optimization_barrier(jnp.sum((pos[:, None] >= ends[None, :]).astype(jnp.int32), axis=1)).astype(jnp.int32)

def low_round(array):
    narrow = lax.optimization_barrier(array.astype(jnp.bfloat16))
    return narrow.astype(jnp.float32)

def sequence_grads(query, key_row, value_row, grad_out, lengths, order):
    scale = 1.0 / math.sqrt(HD)
    pos = positions(order, TOK_DEV // 2, SEQ_LEN)
    doc = documents(pos, lengths)
    allowed = (pos[None, :] <= pos[:, None]) & (doc[None, :] == doc[:, None])
    mask = allowed[:, None, :]
    query3 = query.reshape(SEQ_LEN, HEADS, HD).astype(jnp.float32)
    grad3 = grad_out.reshape(SEQ_LEN, HEADS, HD).astype(jnp.float32)
    key32 = key_row.astype(jnp.float32)
    value32 = value_row.astype(jnp.float32)
    scores = jnp.einsum('ihd,jd->ihj', query3, key32) * scale
    top = lax.optimization_barrier(jnp.max(jnp.where(mask, scores, -1e+30), axis=2, keepdims=True))
    expo = jnp.where(mask, jnp.exp(scores - top), 0.0)
    prob = expo / lax.optimization_barrier(jnp.sum(expo, axis=2, keepdims=True))
    dprob = jnp.einsum('ihd,jd->ihj', grad3, value32)
    delta = lax.optimization_barrier(jnp.sum(prob * dprob, axis=2, keepdims=True))
    dscore = low_round(prob * (dprob - delta))
    prob_low = low_round(prob)
    dquery = jnp.einsum('ihj,jd->ihd', dscore, key32) * scale
    dkey = jnp.einsum('ihj,ihd->jd', dscore, query3) * scale
    dvalue = jnp.einsum('ihj,ihd->jd', prob_low, grad3)
    dkv = jnp.concatenate([dkey, dvalue], axis=1).astype(jnp.bfloat16)
    return (dquery.reshape(SEQ_LEN, HEADS * HD).astype(jnp.bfloat16), dkv)

def adam_blocks(grad, m_codes, m_scales, v_codes, v_scales):
    shape = grad.shape
    g_blocks = grad.reshape(-1, BLOCK)
    m_old = m_codes.reshape(-1, BLOCK).astype(jnp.float32) / 127.0 * m_scales[:, None]
    v_old = v_codes.reshape(-1, BLOCK).astype(jnp.float32) / 255.0 * v_scales[:, None]
    moment = 0.9 * m_old + 0.1 * g_blocks
    second = 0.95 * v_old + 0.05 * g_blocks * g_blocks
    update = moment / (1.0 - 0.9 ** STEP) / (jnp.sqrt(second / (1.0 - 0.95 ** STEP)) + 1e-08)
    m_absmax = lax.optimization_barrier(jnp.max(jnp.abs(moment), axis=1))
    v_absmax = lax.optimization_barrier(jnp.max(second, axis=1))
    m_norm = moment / (m_absmax[:, None] + 1e-06)
    v_norm = second / (v_absmax[:, None] + 1e-06)
    return (update.reshape(shape), m_norm.reshape(shape), m_absmax, v_norm.reshape(shape), v_absmax)

def reference(q_heads, keys, values, out_grad, hidden_in, doc_lengths, span_order, m_codes, m_scales, v_codes, v_scales):

    def one_sequence(total, items):
        query, key_row, value_row, grad_out, layer_in, lengths = items
        dquery, dkv = sequence_grads(query, key_row, value_row, grad_out, lengths, span_order)
        total = total + jnp.dot(layer_in.T, dkv, preferred_element_type=jnp.float32)
        return (total, dquery)
    start = jnp.zeros((D, 2 * HD), jnp.float32)
    grad, dq = lax.scan(one_sequence, start, (q_heads, keys, values, out_grad, hidden_in, doc_lengths))
    update, m_norm, m_absmax, v_norm, v_absmax = adam_blocks(grad, m_codes, m_scales, v_codes, v_scales)
    return (dq, update, m_norm, m_absmax, v_norm, v_absmax)
```

```python
import math

import jax
import jax.numpy as jnp
from jax import lax
from jax.sharding import PartitionSpec as P

BLOCK = 2048
STEP = 10


def positions(order, span, total):
    rows = jnp.arange(total, dtype=jnp.int32)
    slot = rows // span
    match = slot[:, None] == jnp.arange(order.shape[0], dtype=jnp.int32)[None, :]
    first = jnp.sum(jnp.where(match, order[None, :], 0), axis=1)
    return first * span + rows % span


def documents(pos, lengths):
    index = jnp.arange(lengths.shape[0], dtype=jnp.int32)
    ends = jnp.sum(jnp.where(index[None, :] <= index[:, None], lengths[None, :], 0), axis=1)
    return jnp.sum((pos[:, None] >= ends[None, :]).astype(jnp.int32), axis=1)


def adam_blocks(grad, m_codes, m_scales, v_codes, v_scales):
    shape = grad.shape
    g_blocks = grad.reshape(-1, BLOCK)
    m_old = m_codes.reshape(-1, BLOCK).astype(jnp.float32) / 127.0 * m_scales[:, None]
    v_old = v_codes.reshape(-1, BLOCK).astype(jnp.float32) / 255.0 * v_scales[:, None]
    moment = 0.9 * m_old + 0.1 * g_blocks
    second = 0.95 * v_old + 0.05 * g_blocks * g_blocks
    update = moment / (1.0 - 0.9**STEP) / (jnp.sqrt(second / (1.0 - 0.95**STEP)) + 1e-08)
    m_absmax = jnp.max(jnp.abs(moment), axis=1)
    v_absmax = jnp.max(second, axis=1)
    m_norm = moment / (m_absmax[:, None] + 1e-06)
    v_norm = second / (v_absmax[:, None] + 1e-06)
    return (update.reshape(shape), m_norm.reshape(shape), m_absmax, v_norm.reshape(shape), v_absmax)


def contract_rows(left, right):
    return lax.dot_general(
        left, right, (((0,), (0,)), ((), ())), preferred_element_type=jnp.float32
    )


def contract_cols(left, right):
    return lax.dot_general(
        left, right, (((1,), (1,)), ((), ())), preferred_element_type=jnp.float32
    )


def shards(
    q_heads,
    keys,
    values,
    out_grad,
    hidden_in,
    doc_lengths,
    span_order,
    m_codes,
    m_scales,
    v_codes,
    v_scales,
):
    rows = q_heads.shape[1]
    head_dim = keys.shape[2]
    heads_width = q_heads.shape[2]
    nheads = heads_width // head_dim
    scale = 1.0 / math.sqrt(head_dim)
    total = rows * lax.axis_size("ctx")
    key_all, value_all = (
        lax.all_gather(keys[0], "ctx", axis=0, tiled=True),
        lax.all_gather(values[0], "ctx", axis=0, tiled=True),
    )
    pos = positions(span_order, rows // 2, total)
    doc = documents(pos, doc_lengths[0])
    first_row = lax.axis_index("ctx") * rows
    query_pos = lax.dynamic_slice_in_dim(pos, first_row, rows)
    query_doc = lax.dynamic_slice_in_dim(doc, first_row, rows)
    queries = q_heads[0].reshape(rows * nheads, head_dim)
    grads_out = out_grad[0].reshape(rows * nheads, head_dim)
    width = min(512, total)
    nblocks = total // width
    blocks = (
        key_all.reshape(nblocks, width, head_dim),
        value_all.reshape(nblocks, width, head_dim),
        pos.reshape(nblocks, width),
        doc.reshape(nblocks, width),
    )

    def block_masks(key_pos, key_doc):
        small = (key_pos[None, :] <= query_pos[:, None]) & (key_doc[None, :] == query_doc[:, None])
        wide = jnp.broadcast_to(small[:, None, :], (rows, nheads, width)).reshape(
            rows * nheads, width
        )
        return (small, wide)

    def forward_terms(carry, block):
        key_block, value_block, key_pos, key_doc = block
        small, wide = block_masks(key_pos, key_doc)
        top, denom, weighted = carry
        scores = contract_cols(queries, key_block) * scale
        dprob = contract_cols(grads_out, value_block)
        new_top = jnp.maximum(top, jnp.max(jnp.where(wide, scores, -1e30), axis=1, keepdims=True))
        expo = jnp.where(wide, jnp.exp(scores - new_top), 0.0)
        factor = jnp.exp(top - new_top)
        result = (
            new_top,
            denom * factor + jnp.sum(expo, axis=1, keepdims=True),
            weighted * factor + jnp.sum(expo * dprob, axis=1, keepdims=True),
        )
        return (result, None)

    column = jnp.zeros((rows * nheads, 1), jnp.float32)
    start_state = (column - 1e30, column, column)
    (top, denom, weighted), unused = lax.scan(forward_terms, start_state, blocks)
    delta = weighted / denom

    def backward_terms(accum, block):
        key_block, value_block, key_pos, key_doc = block
        small, wide = block_masks(key_pos, key_doc)
        acc = accum
        scores = contract_cols(queries, key_block) * scale
        dprob = contract_cols(grads_out, value_block)
        prob = jnp.where(wide, jnp.exp(scores - top), 0.0) / denom
        prob_low = prob.astype(jnp.bfloat16)
        dscore = (prob * (dprob - delta)).astype(jnp.bfloat16)
        acc = acc + jnp.dot(dscore, key_block, preferred_element_type=jnp.float32)
        dkey = contract_rows(dscore, queries) * scale
        dvalue = contract_rows(prob_low, grads_out)
        return (acc, jnp.concatenate([dkey, dvalue], axis=1))

    dq_sum, pieces = lax.scan(
        backward_terms, jnp.zeros((rows * nheads, head_dim), jnp.float32), blocks
    )
    dq = (dq_sum * scale).reshape(1, rows, heads_width).astype(jnp.bfloat16)
    partial_grads = pieces.reshape(total, 2 * head_dim)
    own = lax.psum_scatter(partial_grads, "ctx", scatter_dimension=0, tiled=True)
    own_low = own.astype(jnp.bfloat16)
    layer_in = hidden_in[0]
    grad = lax.psum_scatter(contract_rows(layer_in, own_low), "dp", scatter_dimension=0, tiled=True)
    grad = lax.psum(grad, "ctx")
    update, m_norm, m_absmax, v_norm, v_absmax = adam_blocks(
        grad, m_codes, m_scales, v_codes, v_scales
    )
    return (dq, update, m_norm, m_absmax, v_norm, v_absmax)


def solution(mesh):
    in_specs = (
        P("dp", "ctx", None),
        P("dp", "ctx", None),
        P("dp", "ctx", None),
        P("dp", "ctx", None),
        P("dp", "ctx", None),
        P("dp", None),
        P(),
        P("dp", None),
        P("dp"),
        P("dp", None),
        P("dp"),
    )
    out_specs = (
        P("dp", "ctx", None),
        P("dp", None),
        P("dp", None),
        P("dp"),
        P("dp", None),
        P("dp"),
    )
    return jax.shard_map(shards, mesh=mesh, in_specs=in_specs, out_specs=out_specs, check_vma=False)
```

```python
import functools
import math

import jax
import jax.numpy as jnp
from jax import lax
from jax.experimental import pallas as pl
from jax.experimental.pallas import tpu as pltpu
from jax.sharding import PartitionSpec as P

STEP = 10
SPAN = 96
WINDOW = 7
HEAD = 128
GROUP = 4
NGROUPS = 4
Z_ORDER = (4, 3, 5, 2, 6, 1, 7, 0)
F32 = jnp.float32
BF16 = jnp.bfloat16
WIRE = jnp.float32
MESH = pl.DeviceIdType.MESH


def remote(src, dst, send, recv, device):
    return pltpu.make_async_remote_copy(
        src_ref=src, dst_ref=dst, send_sem=send, recv_sem=recv, device_id=device, device_id_type=MESH
    )


def greet(devices):
    barrier = pltpu.get_barrier_semaphore()
    for device in devices:
        pl.semaphore_signal(barrier, inc=1, device_id=device, device_id_type=MESH)
    pl.semaphore_wait(barrier, len(devices))


def gather_kernel(k_ref, v_ref, kall, vall, own_sem, send, recv):
    dp, ctx = lax.axis_index("dp"), lax.axis_index("ctx")
    rows = k_ref.shape[0]
    mine = pl.ds(pl.multiple_of(ctx * rows, rows), rows)
    own = [
        pltpu.make_async_copy(k_ref, kall.at[mine], own_sem.at[0]),
        pltpu.make_async_copy(v_ref, vall.at[mine], own_sem.at[1]),
    ]
    for copy in own:
        copy.start()
    peers = [(dp, lax.rem(ctx + o, 8)) for o in range(1, 8)]
    greet(peers)
    copies = []
    for o in (4, 3, 5, 2, 6, 1, 7):
        for which, (src, dst) in enumerate(((k_ref, kall), (v_ref, vall))):
            copy = remote(src, dst.at[mine], send.at[which, o], recv.at[which, o], peers[o - 1])
            copy.start()
            copies.append((copy, which, o, src, dst))
    for copy in own:
        copy.wait()
    for copy, which, o, src, dst in copies:
        copy.wait_send()
        theirs = pl.ds(pl.multiple_of(lax.rem(ctx + 8 - o, 8) * rows, rows), rows)
        remote(src, dst.at[theirs], send.at[which, o], recv.at[which, o], peers[o - 1]).wait_recv()


def gather(keys, values):
    rows, width = keys.shape
    shape = jax.ShapeDtypeStruct((8 * rows, width), keys.dtype)
    any_space = pl.BlockSpec(memory_space=pl.ANY)
    return pl.pallas_call(
        gather_kernel,
        out_shape=[shape, shape],
        in_specs=[any_space] * 2,
        out_specs=[any_space] * 2,
        scratch_shapes=[
            pltpu.SemaphoreType.DMA((2,)),
            pltpu.SemaphoreType.DMA((2, 8)),
            pltpu.SemaphoreType.DMA((2, 8)),
        ],
        compiler_params=pltpu.CompilerParams(collective_id=0, has_side_effects=True),
        name="gather_kv",
    )(keys, values)


def dot_t(left, right):
    return lax.dot_general(left, right, (((1,), (1,)), ((), ())), preferred_element_type=F32)


def attention_kernel(
    order, lens, q_ref, g_ref, kall, vall, dq_ref, dkv_ref,
    inverse, k7, v7, k7t, bias, s_scr, d_scr, p_scr, ds_scr, dk7, dv7, acc,
):
    ctx = lax.axis_index("ctx")
    scale = 1.0 / math.sqrt(HEAD)
    factor = scale * math.log2(math.e)
    width = GROUP * SPAN
    for s in range(16):
        inverse[order[s]] = s
    acc[...] = jnp.zeros_like(acc)

    def query_block(qb, carry):
        place = order[ctx * 2 + qb]
        first = place - (WINDOW - 1)
        stored = [pl.multiple_of(inverse[jnp.maximum(first + r, 0)] * SPAN, SPAN) for r in range(WINDOW)]
        for r in range(WINDOW):
            part = pl.ds(r * SPAN, SPAN)
            k7[part, :] = kall[pl.ds(stored[r], SPAN), :]
            v7[part, :] = vall[pl.ds(stored[r], SPAN), :]
        k7t[...] = k7[...].astype(F32).T.astype(BF16)
        lane = lax.broadcasted_iota(jnp.int32, (1, width), 1)
        head = jnp.zeros_like(lane)
        for h in range(1, GROUP):
            head = head + (lane >= h * SPAN).astype(jnp.int32)
        query_pos = place * SPAN + lane - head * SPAN
        begin = jnp.zeros_like(lane)
        end = jnp.int32(0)
        for k in range(8):
            end = end + lens[0, k]
            begin = jnp.where(query_pos >= end, end, begin)
        for r in range(WINDOW):
            key_pos = (first + r) * SPAN + lax.broadcasted_iota(jnp.int32, (SPAN, width), 0)
            allowed = (key_pos <= query_pos) & (key_pos >= begin)
            bias[pl.ds(r * SPAN, SPAN), :] = jnp.where(allowed, 0.0, -1e30)
        dk7[...] = jnp.zeros_like(dk7)
        dv7[...] = jnp.zeros_like(dv7)
        rows = pl.ds(pl.multiple_of(qb * SPAN, SPAN), SPAN)

        def head_group(grp, carry):
            lanes = [pl.ds(pl.multiple_of(grp * (GROUP * HEAD), GROUP * HEAD) + h * HEAD, HEAD) for h in range(GROUP)]
            queries = jnp.concatenate([q_ref[rows, c] for c in lanes], axis=0)
            cots = jnp.concatenate([g_ref[rows, c] for c in lanes], axis=0)
            top = jnp.full((8, width), -3e38, F32)
            for r in range(WINDOW):
                part = pl.ds(r * SPAN, SPAN)
                scores = dot_t(k7[part, :], queries) + bias[part, :]
                s_scr[part, :] = scores
                d_scr[part, :] = dot_t(v7[part, :], cots)
                top = jnp.maximum(top, jnp.max(scores.reshape(SPAN // 8, 8, width), axis=0))
            top = jnp.max(top, axis=0, keepdims=True)
            denom = jnp.zeros((8, width), F32)
            weighted = jnp.zeros((8, width), F32)
            for r in range(WINDOW):
                part = pl.ds(r * SPAN, SPAN)
                expo = jnp.exp2((s_scr[part, :] - top) * factor)
                s_scr[part, :] = expo
                denom = denom + jnp.sum(expo.reshape(SPAN // 8, 8, width), axis=0)
                weighted = weighted + jnp.sum((expo * d_scr[part, :]).reshape(SPAN // 8, 8, width), axis=0)
            inv = 1.0 / jnp.sum(denom, axis=0, keepdims=True)
            delta = jnp.sum(weighted, axis=0, keepdims=True) * inv
            for r in range(WINDOW):
                part = pl.ds(r * SPAN, SPAN)
                prob = s_scr[part, :] * inv
                p_scr[part, :] = prob.astype(BF16)
                ds_scr[part, :] = (prob * (d_scr[part, :] - delta)).astype(BF16)
            dv7[...] += jnp.dot(p_scr[...], cots, preferred_element_type=F32)
            dk7[...] += jnp.dot(ds_scr[...], queries, preferred_element_type=F32)
            dq = (jnp.dot(k7t[...], ds_scr[...], preferred_element_type=F32) * scale).T.astype(BF16)
            for h in range(GROUP):
                dq_ref[rows, lanes[h]] = dq[h * SPAN : (h + 1) * SPAN, :]
            return carry

        lax.fori_loop(0, 16 // GROUP, head_group, 0)
        for r in range(WINDOW):
            part = pl.ds(r * SPAN, SPAN)
            target = pl.ds(stored[r], SPAN)
            acc[target, 0:HEAD] += dk7[part, :] * scale
            acc[target, HEAD : 2 * HEAD] += dv7[part, :]
        return carry

    lax.fori_loop(0, 2, query_block, 0)
    dkv_ref[...] = acc[...].astype(WIRE)


def attention(order, lens, queries, cots, kall, vall):
    keys = WINDOW * SPAN
    width = GROUP * SPAN
    smem = pl.BlockSpec(memory_space=pltpu.SMEM)
    vmem = pl.BlockSpec(memory_space=pltpu.VMEM)
    return pl.pallas_call(
        attention_kernel,
        out_shape=[
            jax.ShapeDtypeStruct(queries.shape, BF16),
            jax.ShapeDtypeStruct((kall.shape[0], 2 * HEAD), WIRE),
        ],
        in_specs=[smem, smem, vmem, vmem, vmem, vmem],
        out_specs=[vmem, vmem],
        scratch_shapes=[
            pltpu.SMEM((16,), jnp.int32),
            pltpu.VMEM((keys, HEAD), BF16),
            pltpu.VMEM((keys, HEAD), BF16),
            pltpu.VMEM((HEAD, keys), BF16),
            pltpu.VMEM((keys, width), F32),
            pltpu.VMEM((keys, width), F32),
            pltpu.VMEM((keys, width), F32),
            pltpu.VMEM((keys, width), BF16),
            pltpu.VMEM((keys, width), BF16),
            pltpu.VMEM((keys, HEAD), F32),
            pltpu.VMEM((keys, HEAD), F32),
            pltpu.VMEM((kall.shape[0], 2 * HEAD), F32),
        ],
        compiler_params=pltpu.CompilerParams(vmem_limit_bytes=40 * 2**20),
        name="attention_backward",
    )(order, lens, queries, cots, kall, vall)


def reduce_kernel(
    dkv_ref, hid, out_ref,
    held, dkv_in, dkv2, dkvt,
    first, one_in1, two_in1, second, one_in2, two_in2, z_out, z_in, total, gathered,
    hid_own, hid_send, hid_recv, dkv_send, dkv_recv, pair_send, pair_recv,
    send1, recv1, send2, recv2, z_send, z_recv, ag_send, ag_recv,
):
    dp, ctx = lax.axis_index("dp"), lax.axis_index("ctx")
    x, ylo = ctx // 2, lax.rem(ctx, 2)
    z, yhi, core = dp // 4, lax.rem(dp // 2, 2), lax.rem(dp, 2)
    y = yhi * 2 + ylo
    rows = hid.shape[0]

    def at(xx, yy, zz):
        return (zz * 4 + (yy // 2) * 2 + core, xx * 2 + lax.rem(yy, 2))

    x_up, x_down = lax.rem(x + 1, 4), lax.rem(x + 3, 4)
    y_up, y_down = lax.rem(y + 1, 4), lax.rem(y + 3, 4)
    pair = (dp + 1 - 2 * core, ctx)
    ctx_peers = [(dp, lax.rem(ctx + o, 8)) for o in range(1, 8)]
    z_peers = [at(x, y, lax.rem(z + o, 8)) for o in range(1, 8)]
    across = at(x, lax.rem(y + 3 + 2 * ylo, 4), z)

    def columns(slot, c):
        o, yh = Z_ORDER[slot // 2], slot % 2
        block = lax.rem(z + o, 8) * 4 + yh * 2 + c
        return pl.ds(pl.multiple_of(block * 512, 512), 512)

    own = [
        pltpu.make_async_copy(hid.at[:, columns(s, core)], held.at[s, pl.ds(0, rows)], hid_own.at[s])
        for s in range(16)
    ]
    for copy in own:
        copy.start()
    greet([*ctx_peers, *z_peers, pair, across])
    dkv_copies = []
    for o in (4, 3, 5, 2, 6, 1, 7):
        block = pl.ds(pl.multiple_of(lax.rem(ctx + o, 8) * rows, rows), rows)
        copy = remote(dkv_ref.at[block], dkv_in.at[o], dkv_send.at[o], dkv_recv.at[o], ctx_peers[o - 1])
        copy.start()
        dkv_copies.append(copy)
    swaps = []
    for s in range(16):
        copy = remote(
            hid.at[:, columns(s, 1 - core)], held.at[s, pl.ds(rows, rows)], hid_send.at[s], hid_recv.at[s], pair
        )
        copy.start()
        swaps.append(copy)
    for copy in dkv_copies:
        copy.wait()
    total_dkv = dkv_ref[pl.ds(pl.multiple_of(ctx * rows, rows), rows), :].astype(F32)
    for o in range(1, 8):
        total_dkv = total_dkv + dkv_in[o].astype(F32)
    dkv2[pl.ds(0, rows), :] = total_dkv.astype(BF16)
    swap = remote(dkv2.at[pl.ds(0, rows)], dkv2.at[pl.ds(rows, rows)], pair_send, pair_recv, pair)
    swap.start()
    swap.wait()
    dkvt[...] = dkv2[...].astype(F32).T.astype(BF16)

    axes = (
        ((x, at(x_up, y, z), at(x_down, y, z)), (y, at(x, y_up, z), at(x, y_down, z))),
        ((y, at(x, y_up, z), at(x, y_down, z)), (x, at(x_up, y, z), at(x_down, y, z))),
    )
    pending = []

    def ring(stage, part, g):
        place, up, down = axes[part][stage]
        units = 8 if stage == 0 else 2
        half = units // 2
        low, high = pl.ds(0, half), pl.ds(half, half)
        data = (first if stage == 0 else second).at[part, g]
        in1 = (one_in1 if stage == 0 else one_in2).at[part, g]
        in2 = (two_in1 if stage == 0 else two_in2).at[part, g]
        send = (send1 if stage == 0 else send2).at[part, g]
        recv = (recv1 if stage == 0 else recv2).at[part, g]
        after, before, opposite = lax.rem(place + 1, 4), lax.rem(place + 3, 4), lax.rem(place + 2, 4)
        pairs = {
            "a": (data.at[opposite, low], in1.at[0], up),
            "b": (data.at[opposite, high], in1.at[1], down),
            "c": (data.at[after, high], in2.at[0, high], up),
            "d": (data.at[before, low], in2.at[1, low], down),
            "e": (data.at[after, low], in2.at[0, low], up),
            "f": (data.at[before, high], in2.at[1, high], down),
        }

        def copy(name):
            k = "abcdef".index(name)
            src, dst, device = pairs[name]
            return remote(src, dst, send.at[k], recv.at[k], device)

        return dict(
            copy=copy, data=data, in1=in1, in2=in2, low=low, high=high, after=after, before=before, place=place
        )

    def begin(stage, part, g):
        r = ring(stage, part, g)
        for name in "abcd":
            copy = r["copy"](name)
            copy.start()
            pending.append(copy)

    def relay(stage, part, g):
        r = ring(stage, part, g)
        data = r["data"]
        for k, (arrived, sent, place, half) in enumerate((("a", "e", "after", "low"), ("b", "f", "before", "high"))):
            here = (r[place], r[half])
            r["copy"](arrived).wait_recv()
            data[here] = (data[here].astype(F32) + r["in1"][k].astype(F32)).astype(WIRE)
            copy = r["copy"](sent)
            copy.start()
            pending.append(copy)

    def finish(stage, part, g):
        r = ring(stage, part, g)
        for name in "cdef":
            r["copy"](name).wait_recv()
        return r["data"][r["place"]].astype(F32) + r["in2"][0].astype(F32) + r["in2"][1].astype(F32)

    def compute(g):
        for s in range(4 * g, 4 * g + 4):
            own[s].wait()
            swaps[s].wait()

        def block(k, carry):
            j, yh = k // 2, lax.rem(k, 2)
            product = jnp.dot(dkvt[...], held[4 * g + k], preferred_element_type=F32).astype(WIRE)
            for xx in range(4):
                for yl in range(2):
                    r0 = (xx * 2 + yl) * 32
                    yy = yh * 2 + yl
                    first[0, g, xx, yy * 2 + j] = product[r0 : r0 + 32, 0:256]
                    first[1, g, yy, xx * 2 + j] = product[r0 : r0 + 32, 256:512]
            return carry

        lax.fori_loop(0, 4, block, 0)
        for part in range(2):
            begin(0, part, g)

    def middle(g):
        for part in range(2):
            done = finish(0, part, g)
            for t in range(4):
                second[part, g, t] = done[2 * t : 2 * t + 2].astype(WIRE)
            begin(1, part, g)

    def last(g):
        for part in range(2):
            done = finish(1, part, g)
            for j in range(2):
                z_out[2 * g + j, part] = done[j].astype(WIRE)
        for j in range(2):
            o = Z_ORDER[2 * g + j]
            if o:
                copy = remote(z_out.at[2 * g + j], z_in.at[o], z_send.at[o], z_recv.at[o], z_peers[o - 1])
                copy.start()
                pending.append(copy)

    for tick in range(-1, NGROUPS + 4):
        if tick + 1 < NGROUPS:
            compute(tick + 1)
        if 0 <= tick - 3 < NGROUPS:
            last(tick - 3)
        if 0 <= tick - 2 < NGROUPS:
            for part in range(2):
                relay(1, part, tick - 2)
        if 0 <= tick - 1 < NGROUPS:
            middle(tick - 1)
        if 0 <= tick < NGROUPS:
            for part in range(2):
                relay(0, part, tick)

    sums = z_out[Z_ORDER.index(0)].astype(F32)
    for o in (1, 7, 2, 6, 3, 5, 4):
        remote(z_out.at[0], z_in.at[o], z_send.at[o], z_recv.at[o], z_peers[o - 1]).wait_recv()
        sums = sums + z_in[o].astype(F32)
    total[...] = sums
    copies = []
    for o in (4, 3, 5, 2, 6, 1, 7):
        copy = remote(total, gathered.at[o], ag_send.at[o], ag_recv.at[o], ctx_peers[o - 1])
        copy.start()
        copies.append(copy)
    out_ref[ctx] = sums
    for copy in pending:
        copy.wait_send()
    for copy in copies:
        copy.wait()
    for o in range(1, 8):
        out_ref[lax.rem(ctx + 8 - o, 8)] = gathered[o]


def reduce_gradient(dkv, hidden):
    rows = hidden.shape[0]
    dma = pltpu.SemaphoreType.DMA
    unit = (32, 256)
    return pl.pallas_call(
        reduce_kernel,
        out_shape=jax.ShapeDtypeStruct((8, 2, *unit), F32),
        in_specs=[pl.BlockSpec(memory_space=pltpu.VMEM), pl.BlockSpec(memory_space=pl.ANY)],
        out_specs=pl.BlockSpec(memory_space=pltpu.VMEM),
        scratch_shapes=[
            pltpu.VMEM((16, 2 * rows, 512), BF16),
            pltpu.VMEM((8, rows, 256), WIRE),
            pltpu.VMEM((2 * rows, 256), BF16),
            pltpu.VMEM((256, 2 * rows), BF16),
            pltpu.VMEM((2, NGROUPS, 4, 8, *unit), WIRE),
            pltpu.VMEM((2, NGROUPS, 2, 4, *unit), WIRE),
            pltpu.VMEM((2, NGROUPS, 2, 8, *unit), WIRE),
            pltpu.VMEM((2, NGROUPS, 4, 2, *unit), WIRE),
            pltpu.VMEM((2, NGROUPS, 2, 1, *unit), WIRE),
            pltpu.VMEM((2, NGROUPS, 2, 2, *unit), WIRE),
            pltpu.VMEM((8, 2, *unit), WIRE),
            pltpu.VMEM((8, 2, *unit), WIRE),
            pltpu.VMEM((2, *unit), F32),
            pltpu.VMEM((8, 2, *unit), F32),
            dma((16,)), dma((16,)), dma((16,)), dma((8,)), dma((8,)), dma, dma,
            dma((2, NGROUPS, 6)), dma((2, NGROUPS, 6)), dma((2, NGROUPS, 6)), dma((2, NGROUPS, 6)),
            dma((8,)), dma((8,)), dma((8,)), dma((8,)),
        ],
        compiler_params=pltpu.CompilerParams(
            collective_id=1, has_side_effects=True, vmem_limit_bytes=48 * 2**20
        ),
        name="project_and_reduce",
    )(dkv, hidden)


def adam_kernel(grad_t, m_codes, m_scales, v_codes, v_scales, update, m_norm, m_absmax, v_norm, v_absmax, grad):
    for part in range(2):
        grad[pl.ds(part * 256, 256), :] = grad_t[:, part].reshape(256, 256).T

    def block(b, carry):
        rows = pl.ds(pl.multiple_of(b * 8, 8), 8)
        g = grad[rows, :]
        m = 0.9 * (m_codes[rows, :].astype(F32) * (m_scales[b] * (1.0 / 127.0))) + 0.1 * g
        v = 0.95 * (v_codes[rows, :].astype(F32) * (v_scales[b] * (1.0 / 255.0))) + 0.05 * g * g
        update[rows, :] = m * (1.0 / (1.0 - 0.9**STEP)) / (jnp.sqrt(v * (1.0 / (1.0 - 0.95**STEP))) + 1e-08)
        m_top = jnp.max(jnp.abs(m))
        v_top = jnp.max(v)
        m_absmax[b] = m_top
        v_absmax[b] = v_top
        m_norm[rows, :] = m / (m_top + 1e-06)
        v_norm[rows, :] = v / (v_top + 1e-06)
        return carry

    lax.fori_loop(0, 64, block, 0, unroll=8)


def adam(grad_t, m_codes, m_scales, v_codes, v_scales):
    smem = pl.BlockSpec(memory_space=pltpu.SMEM)
    vmem = pl.BlockSpec(memory_space=pltpu.VMEM)
    big = jax.ShapeDtypeStruct(m_codes.shape, F32)
    small = jax.ShapeDtypeStruct(m_scales.shape, F32)
    return pl.pallas_call(
        adam_kernel,
        out_shape=[big, big, small, big, small],
        in_specs=[vmem, vmem, smem, vmem, smem],
        out_specs=[vmem, vmem, smem, vmem, smem],
        scratch_shapes=[pltpu.VMEM(m_codes.shape, F32)],
        compiler_params=pltpu.CompilerParams(vmem_limit_bytes=32 * 2**20),
        name="adam",
    )(grad_t, m_codes, m_scales, v_codes, v_scales)


def shards(
    q_heads, keys, values, out_grad, hidden_in, doc_lengths, span_order, m_codes, m_scales, v_codes, v_scales
):
    kall, vall = gather(keys[0], values[0])
    dq, dkv = attention(span_order, doc_lengths, q_heads[0], out_grad[0], kall, vall)
    grad_t = reduce_gradient(dkv, hidden_in[0])
    update, m_norm, m_absmax, v_norm, v_absmax = adam(grad_t, m_codes, m_scales, v_codes, v_scales)
    return (dq[None], update, m_norm, m_absmax, v_norm, v_absmax)


def solution(mesh):
    in_specs = (
        P("dp", "ctx", None),
        P("dp", "ctx", None),
        P("dp", "ctx", None),
        P("dp", "ctx", None),
        P("dp", "ctx", None),
        P("dp", None),
        P(),
        P("dp", None),
        P("dp"),
        P("dp", None),
        P("dp"),
    )
    out_specs = (
        P("dp", "ctx", None),
        P("dp", None),
        P("dp", None),
        P("dp"),
        P("dp", None),
        P("dp"),
    )
    return jax.shard_map(shards, mesh=mesh, in_specs=in_specs, out_specs=out_specs, check_vma=False)
```

```python
import functools
import math

import jax
import jax.numpy as jnp
from jax import lax
from jax.experimental import pallas as pl
from jax.experimental.pallas import tpu as pltpu
from jax.sharding import PartitionSpec as P

STEP = 10
SPAN = 96
WINDOW = 7
HEAD = 128
GROUP = 4
NGROUPS = 4
FAR_FIRST = (4, 3, 5, 2, 6, 1, 7)
Z_ORDER = (4, 3, 5, 2, 6, 1, 7, 0)
F32 = jnp.float32
BF16 = jnp.bfloat16
MESH = pl.DeviceIdType.MESH


def remote(src, dst, send, recv, device):
    return pltpu.make_async_remote_copy(
        src_ref=src, dst_ref=dst, send_sem=send, recv_sem=recv, device_id=device, device_id_type=MESH
    )


def greet(devices):
    barrier = pltpu.get_barrier_semaphore()
    for device in devices:
        pl.semaphore_signal(barrier, inc=1, device_id=device, device_id_type=MESH)
    pl.semaphore_wait(barrier, len(devices))


def encode(values, message):
    rows = values.shape[0]
    top = jnp.max(jnp.abs(values), axis=0, keepdims=True)
    power = jnp.ceil(jnp.log2(jnp.maximum(top, 1e-30)))
    codes = jnp.round(values * (jnp.exp2(-power) * 32000.0))
    message[pl.ds(0, rows), :] = codes.astype(jnp.int32).astype(jnp.int16)
    head = jnp.broadcast_to(power, (16, values.shape[1]))
    message[pl.ds(rows, 16), :] = head.astype(jnp.int32).astype(jnp.int16)


def decode(message):
    rows = message.shape[0] - 16
    power = message[pl.ds(rows, 16), :].astype(jnp.int32).astype(F32)[0:1, :]
    codes = message[pl.ds(0, rows), :].astype(jnp.int32).astype(F32)
    return codes * (jnp.exp2(power) * (1.0 / 32000.0))


def gather_kernel(k_ref, v_ref, kall, vall, own_sem, send, recv):
    dp, ctx = lax.axis_index("dp"), lax.axis_index("ctx")
    rows = k_ref.shape[0]
    mine = pl.ds(pl.multiple_of(ctx * rows, rows), rows)
    own = [
        pltpu.make_async_copy(k_ref, kall.at[mine], own_sem.at[0]),
        pltpu.make_async_copy(v_ref, vall.at[mine], own_sem.at[1]),
    ]
    for copy in own:
        copy.start()
    peers = [(dp, lax.rem(ctx + o, 8)) for o in range(1, 8)]
    greet(peers)
    copies = []
    for o in (4, 3, 5, 2, 6, 1, 7):
        for which, (src, dst) in enumerate(((k_ref, kall), (v_ref, vall))):
            copy = remote(src, dst.at[mine], send.at[which, o], recv.at[which, o], peers[o - 1])
            copy.start()
            copies.append((copy, which, o, src, dst))
    for copy in own:
        copy.wait()
    for copy, which, o, src, dst in copies:
        copy.wait_send()
        theirs = pl.ds(pl.multiple_of(lax.rem(ctx + 8 - o, 8) * rows, rows), rows)
        remote(src, dst.at[theirs], send.at[which, o], recv.at[which, o], peers[o - 1]).wait_recv()


def gather(keys, values):
    rows, width = keys.shape
    shape = jax.ShapeDtypeStruct((8 * rows, width), keys.dtype)
    any_space = pl.BlockSpec(memory_space=pl.ANY)
    return pl.pallas_call(
        gather_kernel,
        out_shape=[shape, shape],
        in_specs=[any_space] * 2,
        out_specs=[any_space] * 2,
        scratch_shapes=[
            pltpu.SemaphoreType.DMA((2,)),
            pltpu.SemaphoreType.DMA((2, 8)),
            pltpu.SemaphoreType.DMA((2, 8)),
        ],
        compiler_params=pltpu.CompilerParams(collective_id=0, has_side_effects=True),
        name="gather_kv",
    )(keys, values)


def dot_t(left, right):
    return lax.dot_general(left, right, (((1,), (1,)), ((), ())), preferred_element_type=F32)


def attention_kernel(
    order, lens, q_ref, g_ref, kall, vall, dq_ref, dkv_ref,
    inverse, k7, v7, k7t, bias, s_scr, d_scr, p_scr, ds_scr, dk7, dv7, acc,
):
    ctx = lax.axis_index("ctx")
    scale = 1.0 / math.sqrt(HEAD)
    factor = scale * math.log2(math.e)
    width = GROUP * SPAN
    for s in range(16):
        inverse[order[s]] = s
    acc[...] = jnp.zeros_like(acc)

    def query_block(qb, carry):
        place = order[ctx * 2 + qb]
        first = place - (WINDOW - 1)
        stored = [pl.multiple_of(inverse[jnp.maximum(first + r, 0)] * SPAN, SPAN) for r in range(WINDOW)]
        for r in range(WINDOW):
            part = pl.ds(r * SPAN, SPAN)
            k7[part, :] = kall[pl.ds(stored[r], SPAN), :]
            v7[part, :] = vall[pl.ds(stored[r], SPAN), :]
        k7t[...] = k7[...].astype(F32).T.astype(BF16)
        lane = lax.broadcasted_iota(jnp.int32, (1, width), 1)
        head = jnp.zeros_like(lane)
        for h in range(1, GROUP):
            head = head + (lane >= h * SPAN).astype(jnp.int32)
        query_pos = place * SPAN + lane - head * SPAN
        begin = jnp.zeros_like(lane)
        end = jnp.int32(0)
        for k in range(8):
            end = end + lens[0, k]
            begin = jnp.where(query_pos >= end, end, begin)
        for r in range(WINDOW):
            key_pos = (first + r) * SPAN + lax.broadcasted_iota(jnp.int32, (SPAN, width), 0)
            allowed = (key_pos <= query_pos) & (key_pos >= begin)
            bias[pl.ds(r * SPAN, SPAN), :] = jnp.where(allowed, 0.0, -1e30)
        dk7[...] = jnp.zeros_like(dk7)
        dv7[...] = jnp.zeros_like(dv7)
        rows = pl.ds(pl.multiple_of(qb * SPAN, SPAN), SPAN)

        def head_group(grp, carry):
            lanes = [pl.ds(pl.multiple_of(grp * (GROUP * HEAD), GROUP * HEAD) + h * HEAD, HEAD) for h in range(GROUP)]
            queries = jnp.concatenate([q_ref[rows, c] for c in lanes], axis=0)
            cots = jnp.concatenate([g_ref[rows, c] for c in lanes], axis=0)
            top = jnp.full((8, width), -3e38, F32)
            for r in range(WINDOW):
                part = pl.ds(r * SPAN, SPAN)
                scores = dot_t(k7[part, :], queries) + bias[part, :]
                s_scr[part, :] = scores
                d_scr[part, :] = dot_t(v7[part, :], cots)
                top = jnp.maximum(top, jnp.max(scores.reshape(SPAN // 8, 8, width), axis=0))
            top = jnp.max(top, axis=0, keepdims=True)
            denom = jnp.zeros((8, width), F32)
            weighted = jnp.zeros((8, width), F32)
            for r in range(WINDOW):
                part = pl.ds(r * SPAN, SPAN)
                expo = jnp.exp2((s_scr[part, :] - top) * factor)
                s_scr[part, :] = expo
                denom = denom + jnp.sum(expo.reshape(SPAN // 8, 8, width), axis=0)
                weighted = weighted + jnp.sum((expo * d_scr[part, :]).reshape(SPAN // 8, 8, width), axis=0)
            inv = 1.0 / jnp.sum(denom, axis=0, keepdims=True)
            delta = jnp.sum(weighted, axis=0, keepdims=True) * inv
            for r in range(WINDOW):
                part = pl.ds(r * SPAN, SPAN)
                prob = s_scr[part, :] * inv
                p_scr[part, :] = prob.astype(BF16)
                ds_scr[part, :] = (prob * (d_scr[part, :] - delta)).astype(BF16)
            dv7[...] += jnp.dot(p_scr[...], cots, preferred_element_type=F32)
            dk7[...] += jnp.dot(ds_scr[...], queries, preferred_element_type=F32)
            dq = (jnp.dot(k7t[...], ds_scr[...], preferred_element_type=F32) * scale).T.astype(BF16)
            for h in range(GROUP):
                dq_ref[rows, lanes[h]] = dq[h * SPAN : (h + 1) * SPAN, :]
            return carry

        lax.fori_loop(0, 16 // GROUP, head_group, 0)
        for r in range(WINDOW):
            part = pl.ds(r * SPAN, SPAN)
            target = pl.ds(stored[r], SPAN)
            acc[target, 0:HEAD] += dk7[part, :] * scale
            acc[target, HEAD : 2 * HEAD] += dv7[part, :]
        return carry

    lax.fori_loop(0, 2, query_block, 0)
    own = 2 * SPAN

    def write(c, carry):
        encode(acc[pl.ds(pl.multiple_of(c * own, own), own), :], dkv_ref.at[c])
        return carry

    lax.fori_loop(0, 8, write, 0)


def attention(order, lens, queries, cots, kall, vall):
    keys = WINDOW * SPAN
    width = GROUP * SPAN
    smem = pl.BlockSpec(memory_space=pltpu.SMEM)
    vmem = pl.BlockSpec(memory_space=pltpu.VMEM)
    return pl.pallas_call(
        attention_kernel,
        out_shape=[
            jax.ShapeDtypeStruct(queries.shape, BF16),
            jax.ShapeDtypeStruct((8, 2 * SPAN + 16, 2 * HEAD), jnp.int16),
        ],
        in_specs=[smem, smem, vmem, vmem, vmem, vmem],
        out_specs=[vmem, vmem],
        scratch_shapes=[
            pltpu.SMEM((16,), jnp.int32),
            pltpu.VMEM((keys, HEAD), BF16),
            pltpu.VMEM((keys, HEAD), BF16),
            pltpu.VMEM((HEAD, keys), BF16),
            pltpu.VMEM((keys, width), F32),
            pltpu.VMEM((keys, width), F32),
            pltpu.VMEM((keys, width), F32),
            pltpu.VMEM((keys, width), BF16),
            pltpu.VMEM((keys, width), BF16),
            pltpu.VMEM((keys, HEAD), F32),
            pltpu.VMEM((keys, HEAD), F32),
            pltpu.VMEM((kall.shape[0], 2 * HEAD), F32),
        ],
        compiler_params=pltpu.CompilerParams(vmem_limit_bytes=40 * 2**20),
        name="attention_backward",
    )(order, lens, queries, cots, kall, vall)


def reduce_kernel(
    dkv_ref, hid, out_ref,
    held, dkv_in, dkv2, dkvt, first, out1, in1, second, out2, in2, z_out, z_in, ag_out, ag_in,
    hid_own, hid_send, hid_recv, dkv_send, dkv_recv, pair_send, pair_recv,
    send1, recv1, send2, recv2, z_send, z_recv, ag_send, ag_recv,
):
    dp, ctx = lax.axis_index("dp"), lax.axis_index("ctx")
    x, ylo = ctx // 2, lax.rem(ctx, 2)
    z, yhi, core = dp // 4, lax.rem(dp // 2, 2), lax.rem(dp, 2)
    y = yhi * 2 + ylo
    rows = hid.shape[0]

    def at(xx, yy, zz):
        return (zz * 4 + (yy // 2) * 2 + core, xx * 2 + lax.rem(yy, 2))

    x_ring = (x, at(lax.rem(x + 1, 4), y, z), at(lax.rem(x + 3, 4), y, z))
    y_ring = (y, at(x, lax.rem(y + 1, 4), z), at(x, lax.rem(y + 3, 4), z))
    pair = (dp + 1 - 2 * core, ctx)
    ctx_peers = [(dp, lax.rem(ctx + o, 8)) for o in range(1, 8)]
    z_peers = [at(x, y, lax.rem(z + o, 8)) for o in range(1, 8)]
    across = at(x, lax.rem(y + 3 + 2 * ylo, 4), z)

    def columns(slot, c):
        o, yh = Z_ORDER[slot // 2], slot % 2
        block = lax.rem(z + o, 8) * 4 + yh * 2 + c
        return pl.ds(pl.multiple_of(block * 512, 512), 512)

    own = [
        pltpu.make_async_copy(hid.at[:, columns(s, core)], held.at[s, pl.ds(0, rows)], hid_own.at[s])
        for s in range(16)
    ]
    for copy in own:
        copy.start()
    greet([*ctx_peers, *z_peers, pair, across])
    dkv_copies = []
    for o in FAR_FIRST:
        copy = remote(
            dkv_ref.at[lax.rem(ctx + o, 8)], dkv_in.at[o], dkv_send.at[o], dkv_recv.at[o], ctx_peers[o - 1]
        )
        copy.start()
        dkv_copies.append(copy)
    swaps = []
    for s in range(16):
        copy = remote(
            hid.at[:, columns(s, 1 - core)], held.at[s, pl.ds(rows, rows)], hid_send.at[s], hid_recv.at[s], pair
        )
        copy.start()
        swaps.append(copy)
    for copy in dkv_copies:
        copy.wait()
    total_dkv = decode(dkv_ref.at[ctx])
    for o in range(1, 8):
        total_dkv = total_dkv + decode(dkv_in.at[o])
    dkv2[pl.ds(0, rows), :] = total_dkv.astype(BF16)
    swap = remote(dkv2.at[pl.ds(0, rows)], dkv2.at[pl.ds(rows, rows)], pair_send, pair_recv, pair)
    swap.start()
    swap.wait()
    dkvt[...] = dkv2[...].astype(F32).T.astype(BF16)

    rings = ((x_ring, y_ring), (y_ring, x_ring))
    stages = ((first, out1, in1, send1, recv1, 4), (second, out2, in2, send2, recv2, 1))
    pending = []

    def piece(stage, part, g, place, high):
        data, half = stages[stage][0], stages[stage][5]
        return data.at[part, g, place, pl.ds(half * high, half)]

    def flat(value):
        return value.reshape(-1, 128)

    def copy_of(stage, part, g, k):
        data, out, into, send, recv, half = stages[stage]
        up = k % 2 == 0
        device = rings[part][stage][1 if up else 2]
        return remote(out.at[part, g, k], into.at[part, g, k], send.at[part, g, k], recv.at[part, g, k], device)

    def post(stage, part, g, k, value):
        encode(value, stages[stage][1].at[part, g, k])
        copy = copy_of(stage, part, g, k)
        copy.start()
        pending.append(copy)

    def arrived(stage, part, g, k):
        copy_of(stage, part, g, k).wait_recv()
        return decode(stages[stage][2].at[part, g, k])

    def begin(stage, part, g):
        place = rings[part][stage][0]
        after, before, opposite = lax.rem(place + 1, 4), lax.rem(place + 3, 4), lax.rem(place + 2, 4)
        for k, (owner, high) in enumerate(((opposite, 0), (opposite, 1), (after, 1), (before, 0))):
            post(stage, part, g, k, flat(piece(stage, part, g, owner, high)[...]))

    def relay(stage, part, g):
        place = rings[part][stage][0]
        after, before = lax.rem(place + 1, 4), lax.rem(place + 3, 4)
        for k, (owner, high) in enumerate(((after, 0), (before, 1))):
            value = arrived(stage, part, g, k) + flat(piece(stage, part, g, owner, high)[...])
            post(stage, part, g, 4 + k, value)

    def finish(stage, part, g):
        place = rings[part][stage][0]
        low = arrived(stage, part, g, 3) + arrived(stage, part, g, 4)
        high = arrived(stage, part, g, 2) + arrived(stage, part, g, 5)
        low = low + flat(piece(stage, part, g, place, 0)[...])
        high = high + flat(piece(stage, part, g, place, 1)[...])
        return low, high

    def compute(g):
        for s in range(4 * g, 4 * g + 4):
            own[s].wait()
            swaps[s].wait()

        def block(k, carry):
            j, yh = k // 2, lax.rem(k, 2)
            product = jnp.dot(dkvt[...], held[4 * g + k], preferred_element_type=F32)
            for xx in range(4):
                for yl in range(2):
                    r0 = (xx * 2 + yl) * 32
                    yy = yh * 2 + yl
                    for side in range(2):
                        first[0, g, xx, yy * 2 + j, side] = product[r0 : r0 + 32, side * 128 : side * 128 + 128]
                        first[1, g, yy, xx * 2 + j, side] = product[r0 : r0 + 32, side * 128 + 256 : side * 128 + 384]
            return carry

        lax.fori_loop(0, 4, block, 0)
        for part in range(2):
            begin(0, part, g)

    def middle(g):
        for part in range(2):
            low, high = finish(0, part, g)
            for t in range(4):
                half = (low, high)[t // 2].reshape(2, 2, 2, 32, 128)
                second[part, g, t] = half[t % 2]
            begin(1, part, g)

    def last(g):
        parts = [finish(1, part, g) for part in range(2)]
        for j in range(2):
            slot = 2 * g + j
            value = jnp.concatenate([parts[0][j], parts[1][j]], axis=0)
            o = Z_ORDER[slot]
            if o == 0:
                return value
            encode(value, z_out.at[slot])
            copy = remote(z_out.at[slot], z_in.at[o], z_send.at[o], z_recv.at[o], z_peers[o - 1])
            copy.start()
            pending.append(copy)

    for tick in range(-1, NGROUPS + 3):
        if tick + 1 < NGROUPS:
            compute(tick + 1)
        if 0 <= tick - 3 < NGROUPS:
            sums = last(tick - 3)
        if 0 <= tick - 2 < NGROUPS:
            for part in range(2):
                relay(1, part, tick - 2)
        if 0 <= tick - 1 < NGROUPS:
            middle(tick - 1)
        if 0 <= tick < NGROUPS:
            for part in range(2):
                relay(0, part, tick)

    for o in (1, 7, 2, 6, 3, 5, 4):
        remote(z_out.at[0], z_in.at[o], z_send.at[o], z_recv.at[o], z_peers[o - 1]).wait_recv()
        sums = sums + decode(z_in.at[o])
    encode(sums, ag_out)
    copies = []
    for o in FAR_FIRST:
        copy = remote(ag_out, ag_in.at[o], ag_send.at[o], ag_recv.at[o], ctx_peers[o - 1])
        copy.start()
        copies.append(copy)
    out_ref[ctx] = decode(ag_out).reshape(4, 32, 128)
    for copy in pending:
        copy.wait_send()
    for copy in copies:
        copy.wait()
    for o in range(1, 8):
        out_ref[lax.rem(ctx + 8 - o, 8)] = decode(ag_in.at[o]).reshape(4, 32, 128)


def reduce_gradient(dkv, hidden):
    rows = hidden.shape[0]
    dma = pltpu.SemaphoreType.DMA
    codes = jnp.int16
    return pl.pallas_call(
        reduce_kernel,
        out_shape=jax.ShapeDtypeStruct((8, 4, 32, 128), F32),
        in_specs=[pl.BlockSpec(memory_space=pltpu.VMEM), pl.BlockSpec(memory_space=pl.ANY)],
        out_specs=pl.BlockSpec(memory_space=pltpu.VMEM),
        scratch_shapes=[
            pltpu.VMEM((16, 2 * rows, 512), BF16),
            pltpu.VMEM((8, rows + 16, 256), codes),
            pltpu.VMEM((2 * rows, 256), BF16),
            pltpu.VMEM((256, 2 * rows), BF16),
            pltpu.VMEM((2, NGROUPS, 4, 8, 2, 32, 128), F32),
            pltpu.VMEM((2, NGROUPS, 6, 272, 128), codes),
            pltpu.VMEM((2, NGROUPS, 6, 272, 128), codes),
            pltpu.VMEM((2, NGROUPS, 4, 2, 2, 32, 128), F32),
            pltpu.VMEM((2, NGROUPS, 6, 80, 128), codes),
            pltpu.VMEM((2, NGROUPS, 6, 80, 128), codes),
            pltpu.VMEM((8, 144, 128), codes),
            pltpu.VMEM((8, 144, 128), codes),
            pltpu.VMEM((144, 128), codes),
            pltpu.VMEM((8, 144, 128), codes),
            dma((16,)), dma((16,)), dma((16,)), dma((8,)), dma((8,)), dma, dma,
            dma((2, NGROUPS, 6)), dma((2, NGROUPS, 6)), dma((2, NGROUPS, 6)), dma((2, NGROUPS, 6)),
            dma((8,)), dma((8,)), dma((8,)), dma((8,)),
        ],
        compiler_params=pltpu.CompilerParams(
            collective_id=1, has_side_effects=True, vmem_limit_bytes=48 * 2**20
        ),
        name="project_and_reduce",
    )(dkv, hidden)


def adam_kernel(grad_t, m_codes, m_scales, v_codes, v_scales, update, m_norm, m_absmax, v_norm, v_absmax, grad):
    for q in range(4):
        grad[pl.ds(q * 128, 128), :] = grad_t[:, q].reshape(256, 128).T

    def block(b, carry):
        rows = pl.ds(pl.multiple_of(b * 8, 8), 8)
        g = grad[rows, :]
        m = 0.9 * (m_codes[rows, :].astype(F32) * (m_scales[b] * (1.0 / 127.0))) + 0.1 * g
        v = 0.95 * (v_codes[rows, :].astype(F32) * (v_scales[b] * (1.0 / 255.0))) + 0.05 * g * g
        update[rows, :] = m * (1.0 / (1.0 - 0.9**STEP)) / (jnp.sqrt(v * (1.0 / (1.0 - 0.95**STEP))) + 1e-08)
        m_top = jnp.max(jnp.abs(m))
        v_top = jnp.max(v)
        m_absmax[b] = m_top
        v_absmax[b] = v_top
        m_norm[rows, :] = m / (m_top + 1e-06)
        v_norm[rows, :] = v / (v_top + 1e-06)
        return carry

    lax.fori_loop(0, 64, block, 0, unroll=8)


def adam(grad_t, m_codes, m_scales, v_codes, v_scales):
    smem = pl.BlockSpec(memory_space=pltpu.SMEM)
    vmem = pl.BlockSpec(memory_space=pltpu.VMEM)
    big = jax.ShapeDtypeStruct(m_codes.shape, F32)
    small = jax.ShapeDtypeStruct(m_scales.shape, F32)
    return pl.pallas_call(
        adam_kernel,
        out_shape=[big, big, small, big, small],
        in_specs=[vmem, vmem, smem, vmem, smem],
        out_specs=[vmem, vmem, smem, vmem, smem],
        scratch_shapes=[pltpu.VMEM(m_codes.shape, F32)],
        compiler_params=pltpu.CompilerParams(vmem_limit_bytes=32 * 2**20),
        name="adam",
    )(grad_t, m_codes, m_scales, v_codes, v_scales)


def shards(
    q_heads, keys, values, out_grad, hidden_in, doc_lengths, span_order, m_codes, m_scales, v_codes, v_scales
):
    kall, vall = gather(keys[0], values[0])
    dq, dkv = attention(span_order, doc_lengths, q_heads[0], out_grad[0], kall, vall)
    grad_t = reduce_gradient(dkv, hidden_in[0])
    update, m_norm, m_absmax, v_norm, v_absmax = adam(grad_t, m_codes, m_scales, v_codes, v_scales)
    return (dq[None], update, m_norm, m_absmax, v_norm, v_absmax)


def solution(mesh):
    in_specs = (
        P("dp", "ctx", None),
        P("dp", "ctx", None),
        P("dp", "ctx", None),
        P("dp", "ctx", None),
        P("dp", "ctx", None),
        P("dp", None),
        P(),
        P("dp", None),
        P("dp"),
        P("dp", None),
        P("dp"),
    )
    out_specs = (
        P("dp", "ctx", None),
        P("dp", None),
        P("dp", None),
        P("dp"),
        P("dp", None),
        P("dp"),
    )
    return jax.shard_map(shards, mesh=mesh, in_specs=in_specs, out_specs=out_specs, check_vma=False)
```

```python
import functools
import math

import jax
import jax.numpy as jnp
from jax import lax
from jax.experimental import pallas as pl
from jax.experimental.pallas import tpu as pltpu
from jax.sharding import PartitionSpec as P

STEP = 10
SPAN = 96
WINDOW = 7
HEAD = 128
GROUP = 8
NGROUPS = 2
FAR_FIRST = (4, 3, 5, 2, 6, 1, 7)
DISTANCES = ((4, 2), (0, 6))
F32 = jnp.float32
BF16 = jnp.bfloat16
MESH = pl.DeviceIdType.MESH


def remote(src, dst, send, recv, device):
    return pltpu.make_async_remote_copy(
        src_ref=src, dst_ref=dst, send_sem=send, recv_sem=recv, device_id=device, device_id_type=MESH
    )


def greet(devices):
    barrier = pltpu.get_barrier_semaphore()
    for device in devices:
        pl.semaphore_signal(barrier, inc=1, device_id=device, device_id_type=MESH)
    pl.semaphore_wait(barrier, len(devices))


def encode(values, message):
    rows = values.shape[0]
    top = jnp.max(jnp.abs(values), axis=0, keepdims=True)
    power = jnp.ceil(jnp.log2(jnp.maximum(top, 1e-30)))
    codes = jnp.round(values * (jnp.exp2(-power) * 32000.0))
    message[pl.ds(0, rows), :] = codes.astype(jnp.int32).astype(jnp.int16)
    head = jnp.broadcast_to(power, (16, values.shape[1]))
    message[pl.ds(rows, 16), :] = head.astype(jnp.int32).astype(jnp.int16)


def decode(message):
    rows = message.shape[0] - 16
    power = message[pl.ds(rows, 16), :].astype(jnp.int32).astype(F32)[0:1, :]
    codes = message[pl.ds(0, rows), :].astype(jnp.int32).astype(F32)
    return codes * (jnp.exp2(power) * (1.0 / 32000.0))


def dot_t(left, right):
    return lax.dot_general(left, right, (((1,), (1,)), ((), ())), preferred_element_type=F32)


def window_of(order, place, stored, window):
    def pick(r, carry):
        wanted = place - (WINDOW - 1) + r
        block = jnp.zeros((SPAN, HEAD), BF16)
        for s in range(16):
            weight = jnp.where(order[s] == wanted, 1.0, 0.0).astype(BF16)
            block = block + stored[pl.ds(s * SPAN, SPAN), :] * weight
        window[pl.ds(pl.multiple_of(r * SPAN, SPAN), SPAN), :] = block
        return carry

    lax.fori_loop(0, WINDOW, pick, 0)


def mask_bias(place, lens, bias):
    width = GROUP * SPAN
    lane = lax.broadcasted_iota(jnp.int32, (1, width), 1)
    head = jnp.zeros_like(lane)
    for h in range(1, GROUP):
        head = head + (lane >= h * SPAN).astype(jnp.int32)
    query_pos = place * SPAN + lane - head * SPAN
    begin = jnp.zeros_like(lane)
    end = jnp.int32(0)
    for k in range(8):
        end = end + lens[0, k]
        begin = jnp.where(query_pos >= end, end, begin)
    for r in range(WINDOW):
        key_pos = (place - (WINDOW - 1) + r) * SPAN + lax.broadcasted_iota(jnp.int32, (SPAN, width), 0)
        allowed = (key_pos <= query_pos) & (key_pos >= begin)
        bias[pl.ds(r * SPAN, SPAN), :] = jnp.where(allowed, 0.0, -1e30)


def heads_of(ref, qb, grp):
    rows = pl.ds(pl.multiple_of(qb * SPAN, SPAN), SPAN)
    wide = GROUP * HEAD
    lanes = [pl.ds(pl.multiple_of(grp * wide, wide) + h * HEAD, HEAD) for h in range(GROUP)]
    return rows, lanes, jnp.concatenate([ref[rows, c] for c in lanes], axis=0)


def softmax_numerators(k7, queries, bias, expo_scr, inv_scr):
    factor = math.log2(math.e) / math.sqrt(HEAD)
    width = GROUP * SPAN
    parts = [pl.ds(r * SPAN, SPAN) for r in range(WINDOW)]
    expo_scr[...] = dot_t(k7[...], queries)
    top = jnp.full((8, width), -3e38, F32)
    for part in parts:
        scores = expo_scr[part, :] + bias[part, :]
        expo_scr[part, :] = scores
        top = jnp.maximum(top, jnp.max(scores.reshape(SPAN // 8, 8, width), axis=0))
    top = jnp.max(top, axis=0, keepdims=True)
    denom = jnp.zeros((8, width), F32)
    for part in parts:
        expo = jnp.exp2((expo_scr[part, :] - top) * factor)
        expo_scr[part, :] = expo
        denom = denom + jnp.sum(expo.reshape(SPAN // 8, 8, width), axis=0)
    inv_scr[...] = jnp.broadcast_to(1.0 / jnp.sum(denom, axis=0, keepdims=True), (8, width))


def softmax_terms(v7, cots, expo_scr, inv_scr, d_scr, p_scr, ds_scr):
    width = GROUP * SPAN
    parts = [pl.ds(r * SPAN, SPAN) for r in range(WINDOW)]
    d_scr[...] = dot_t(v7[...], cots)
    inv = inv_scr[0:1, :]
    weighted = jnp.zeros((8, width), F32)
    for part in parts:
        prob = expo_scr[part, :] * inv
        expo_scr[part, :] = prob
        p_scr[part, :] = prob.astype(BF16)
        weighted = weighted + jnp.sum((prob * d_scr[part, :]).reshape(SPAN // 8, 8, width), axis=0)
    delta = jnp.sum(weighted, axis=0, keepdims=True)
    for part in parts:
        ds_scr[part, :] = (expo_scr[part, :] * (d_scr[part, :] - delta)).astype(BF16)


def messages(order, places, found, out, gain):
    def write(c, carry):
        halves = []
        for half in range(2):
            place = order[2 * c + half]
            value = jnp.zeros((SPAN, HEAD), F32)
            for qb in range(2):
                for r in range(WINDOW):
                    weight = jnp.where(place - (places[qb] - (WINDOW - 1)) == r, 1.0, 0.0)
                    value = value + found[qb, pl.ds(r * SPAN, SPAN), :] * weight
            halves.append(value)
        encode(jnp.concatenate(halves, axis=0) * gain, out.at[c])
        return carry

    lax.fori_loop(0, 8, write, 0)


def backward_kernel(
    order, lens, q_hbm, g_hbm, k_hbm, v_hbm, hid, dq_hbm, out_ref,
    q_ref, g_ref, kall, vall, k7, v7, k7t, bias, expo_all, inv_all, d_scr, p_scr, ds_all, dkw, dvw, dk_out, dv_out, dk_in, dv_in, dq_ref,
    load_sem, kv_send, kv_recv, dk_send, dk_recv, dv_send, dv_recv,
    held, dkv2, dkvt, first, out1, in1, second, out2, in2, z_out, z_in, total, ag_out, ag_in,
    hid_own, hid_send, hid_recv, near_send, near_recv, pair_send, pair_recv,
    send1, recv1, send2, recv2, z_send, z_recv, ag_send, ag_recv,
):
    dp, ctx = lax.axis_index("dp"), lax.axis_index("ctx")
    x, ylo = ctx // 2, lax.rem(ctx, 2)
    z, yhi, core = dp // 4, lax.rem(dp // 2, 2), lax.rem(dp, 2)
    y = yhi * 2 + ylo
    rows = hid.shape[0]

    def at(xx, yy, zz):
        return (zz * 4 + (yy // 2) * 2 + core, xx * 2 + lax.rem(yy, 2))

    x_ring = (x, *[at(lax.rem(x + k, 4), y, z) for k in range(1, 4)])
    y_ring = (y, *[at(x, lax.rem(y + k, 4), z) for k in range(1, 4)])
    pair = (dp + 1 - 2 * core, ctx)
    ctx_peers = [(dp, lax.rem(ctx + o, 8)) for o in range(1, 8)]
    even_peers = [at(x, y, lax.rem(z + o, 8)) for o in (2, 4, 6)]
    y_far = at(x, lax.rem(y + 2, 4), z)
    across = at(x, lax.rem(y + 3 + 2 * ylo, 4), z)

    def columns(zz, kind, j, yh, c):
        distance = 4 - 4 * j + kind * (8 * j - 2)
        block = lax.rem(zz + distance, 8) * 4 + yh * 2 + c
        return pl.ds(pl.multiple_of(block * 512, 512), 512)

    parity = lax.rem(z, 2)
    wanted = lax.rem(z, 4) // 2
    near = []
    for n in range(2):
        zz = lax.rem(z + (1 - 2 * n) * (1 - 2 * parity) + 8, 8)
        for c in range(2):
            near.append((zz, lax.rem(core + c, 2)))
    sharers = [(zz * 4 + yhi * 2 + cc, ctx) for zz, cc in near]

    mine = pl.ds(pl.multiple_of(ctx * rows, rows), rows)
    loads = [
        pltpu.make_async_copy(src, dst, load_sem.at[k])
        for k, (src, dst) in enumerate(
            ((k_hbm, kall.at[mine]), (v_hbm, vall.at[mine]), (q_hbm, q_ref), (g_hbm, g_ref))
        )
    ]
    for copy in loads:
        copy.start()
    greet([*ctx_peers, *even_peers, *sharers, pair, across, y_far])
    kv_copies = []
    for which, (src, dst) in enumerate(((k_hbm, kall), (v_hbm, vall))):
        for o in FAR_FIRST:
            copy = remote(src, dst.at[mine], kv_send.at[which, o], kv_recv.at[which, o], ctx_peers[o - 1])
            copy.start()
            kv_copies.append(copy)
    near_copies = []
    for j in range(2):
        for yh in range(2):
            for n, (zz, cc) in enumerate(near):
                slot, block = j * 4 + wanted * 2 + yh, 2 + n % 2
                copy = remote(
                    hid.at[:, columns(zz, wanted, j, yh, cc)],
                    held.at[slot, pl.ds(block * rows, rows)],
                    near_send.at[j * 2 + yh, n],
                    near_recv.at[slot, n % 2],
                    sharers[n],
                )
                copy.start()
                near_copies.append(copy)
    own, swaps = [], []
    for slot in range(8):
        j, kind, yh = slot // 4, slot // 2 % 2, slot % 2
        own.append(
            pltpu.make_async_copy(
                hid.at[:, columns(z, kind, j, yh, core)], held.at[slot, pl.ds(0, rows)], hid_own.at[slot]
            )
        )
        own[slot].start()
        copy = remote(
            hid.at[:, columns(z, kind, j, yh, 1 - core)],
            held.at[slot, pl.ds(rows, rows)],
            hid_send.at[slot],
            hid_recv.at[slot],
            pair,
        )
        copy.start()
        swaps.append(copy)

    places = [order[2 * ctx], order[2 * ctx + 1]]
    for qb in range(2):
        mask_bias(places[qb], lens, bias.at[qb])
    dvw[...] = jnp.zeros_like(dvw)
    dkw[...] = jnp.zeros_like(dkw)
    def all_here(which, src, dst):
        loads[which].wait()
        for o in FAR_FIRST:
            theirs = pl.ds(pl.multiple_of(lax.rem(ctx + 8 - o, 8) * rows, rows), rows)
            remote(src, dst.at[theirs], kv_send.at[which, o], kv_recv.at[which, o], ctx_peers[o - 1]).wait_recv()

    reach = pl.ds(0, WINDOW * SPAN)
    steps = 2 * 16 // GROUP
    scale = 1.0 / math.sqrt(HEAD)
    all_here(0, k_hbm, kall)
    loads[2].wait()
    for qb in range(2):
        window_of(order, places[qb], kall, k7.at[qb])

    def numerator_step(it, carry):
        qb, grp = it // (steps // 2), lax.rem(it, steps // 2)
        queries = heads_of(q_ref, qb, grp)[2]
        softmax_numerators(k7.at[qb], queries, bias.at[qb], expo_all.at[it], inv_all.at[it])
        return carry

    lax.fori_loop(0, steps, numerator_step, 0)
    all_here(1, v_hbm, vall)
    loads[3].wait()
    for qb in range(2):
        window_of(order, places[qb], vall, v7.at[qb])

    def score_step(it, carry):
        qb, grp = it // (steps // 2), lax.rem(it, steps // 2)
        cots = heads_of(g_ref, qb, grp)[2]
        softmax_terms(v7.at[qb], cots, expo_all.at[it], inv_all.at[it], d_scr, p_scr, ds_all.at[it])
        dvw[qb, reach, :] += jnp.dot(p_scr[...], cots, preferred_element_type=F32)
        return carry

    lax.fori_loop(0, steps, score_step, 0)

    def exchange(out, into, send, recv):
        copies = []
        for o in FAR_FIRST:
            copy = remote(out.at[lax.rem(ctx + o, 8)], into.at[o], send.at[o], recv.at[o], ctx_peers[o - 1])
            copy.start()
            copies.append(copy)
        return copies

    messages(order, places, dvw, dv_out, 1.0)
    dv_copies = exchange(dv_out, dv_in, dv_send, dv_recv)

    def key_step(it, carry):
        qb, grp = it // (steps // 2), lax.rem(it, steps // 2)
        queries = heads_of(q_ref, qb, grp)[2]
        dkw[qb, reach, :] += jnp.dot(ds_all[it], queries, preferred_element_type=F32)
        return carry

    lax.fori_loop(0, steps, key_step, 0)
    messages(order, places, dkw, dk_out, scale)
    dk_copies = exchange(dk_out, dk_in, dk_send, dk_recv)

    for qb in range(2):
        k7t[qb] = k7[qb].astype(F32).T.astype(BF16)

    def query_step(it, carry):
        qb, grp = it // (steps // 2), lax.rem(it, steps // 2)
        query_rows, lanes, _ = heads_of(q_ref, qb, grp)
        dq = (jnp.dot(k7t[qb], ds_all[it], preferred_element_type=F32) * scale).T.astype(BF16)
        for h in range(GROUP):
            dq_ref[query_rows, lanes[h]] = dq[h * SPAN : (h + 1) * SPAN, :]
        return carry

    lax.fori_loop(0, steps, query_step, 0)
    dq_copy = pltpu.make_async_copy(dq_ref, dq_hbm, load_sem.at[4])
    dq_copy.start()

    dkv_copies = []
    for side, (copies, out, into) in enumerate(((dk_copies, dk_out, dk_in), (dv_copies, dv_out, dv_in))[::-1]):
        for copy in copies:
            copy.wait()
        value = decode(out.at[ctx])
        for o in range(1, 8):
            value = value + decode(into.at[o])
        lanes = pl.ds((1 - side) * HEAD, HEAD)
        dkv2[pl.ds(0, rows), lanes] = value.astype(BF16)
        for n, device in enumerate([pair, *sharers]):
            start, arrival = rows, 0
            if n:
                arrival = 1 + 2 * wanted + (n - 1) % 2
                start = (1 + arrival) * rows
            copy = remote(
                dkv2.at[pl.ds(0, rows), lanes],
                dkv2.at[pl.ds(pl.multiple_of(start, rows), rows), lanes],
                pair_send.at[side, n],
                pair_recv.at[side, arrival],
                device,
            )
            copy.start()
            dkv_copies.append(copy)
    for side in range(2):
        for n in range(5):
            lanes = pl.ds((1 - side) * HEAD, HEAD)
            remote(
                dkv2.at[pl.ds(0, rows), lanes],
                dkv2.at[pl.ds((1 + n) * rows, rows), lanes],
                pair_send.at[side, n],
                pair_recv.at[side, n],
                pair,
            ).wait_recv()
    dkvt[...] = dkv2[...].astype(F32).T.astype(BF16)

    rings = ((x_ring, y_ring), (y_ring, x_ring))
    pending = []

    def flat(value):
        return value.reshape(-1, 128)

    def piece(part, g, place, high):
        return flat(first[part, g, place, pl.ds(4 * high, 4)])

    def copy_of(part, g, k):
        device = rings[part][0][1 if k % 2 == 0 else 3]
        return remote(out1.at[part, g, k], in1.at[part, g, k], send1.at[part, g, k], recv1.at[part, g, k], device)

    def post(part, g, k, value):
        encode(value, out1.at[part, g, k])
        copy = copy_of(part, g, k)
        copy.start()
        pending.append(copy)

    def arrived(part, g, k):
        copy_of(part, g, k).wait_recv()
        return decode(in1.at[part, g, k])

    def begin(part, g):
        place = rings[part][0][0]
        after, before, opposite = lax.rem(place + 1, 4), lax.rem(place + 3, 4), lax.rem(place + 2, 4)
        for k, (owner, high) in enumerate(((opposite, 0), (opposite, 1), (after, 1), (before, 0))):
            post(part, g, k, piece(part, g, owner, high))

    def relay(part, g):
        place = rings[part][0][0]
        after, before = lax.rem(place + 1, 4), lax.rem(place + 3, 4)
        for k, (owner, high) in enumerate(((after, 0), (before, 1))):
            post(part, g, 4 + k, arrived(part, g, k) + piece(part, g, owner, high))

    def finish(part, g):
        place = rings[part][0][0]
        low = arrived(part, g, 3) + arrived(part, g, 4) + piece(part, g, place, 0)
        high = arrived(part, g, 2) + arrived(part, g, 5) + piece(part, g, place, 1)
        return low, high

    def direct(part, g, k):
        return remote(
            out2.at[part, g, k], in2.at[part, g, k], send2.at[part, g, k], recv2.at[part, g, k], rings[part][1][k]
        )

    def compute(g):
        for slot in range(4 * g, 4 * g + 4):
            own[slot].wait()
            swaps[slot].wait()
            for c in range(2):
                block = pl.ds((2 + c) * rows, rows)
                remote(
                    hid.at[:, pl.ds(0, 512)], held.at[slot, block], near_send.at[0, 0], near_recv.at[slot, c], pair
                ).wait_recv()

        def block(k, carry):
            kind, yh = k // 2, lax.rem(k, 2)
            theirs = pl.ds(pl.multiple_of(2 * rows * (1 + kind), 128), 2 * rows)
            here, both = pl.ds(0, 2 * rows), pl.ds(2 * rows, 2 * rows)
            product = jnp.dot(dkvt[:, 0 : 2 * rows], held[4 * g + k, here], preferred_element_type=F32)
            product = product + jnp.dot(
                dkvt[:, theirs], held[4 * g + k, both], preferred_element_type=F32
            )
            for xx in range(4):
                for yl in range(2):
                    r0 = (xx * 2 + yl) * 32
                    yy = yh * 2 + yl
                    for side in range(2):
                        first[0, g, xx, yy * 2 + kind, side] = product[r0 : r0 + 32, side * 128 : side * 128 + 128]
                        first[1, g, yy, xx * 2 + kind, side] = product[r0 : r0 + 32, side * 128 + 256 : side * 128 + 384]
            return carry

        lax.fori_loop(0, 4, block, 0)
        for part in range(2):
            begin(part, g)

    def middle(g):
        for part in range(2):
            low, high = finish(part, g)
            for t in range(4):
                half = (low, high)[t // 2].reshape(2, 2, 2, 32, 128)
                second[part, g, t] = half[t % 2]
            place = rings[part][1][0]
            for k in (2, 1, 3):
                encode(flat(second[part, g, lax.rem(place + k, 4)]), out2.at[part, g, k])
                copy = direct(part, g, k)
                copy.start()
                pending.append(copy)

    def last(g):
        parts = []
        for part in range(2):
            value = flat(second[part, g, rings[part][1][0]])
            for k in (1, 3, 2):
                direct(part, g, k).wait_recv()
                value = value + decode(in2.at[part, g, k])
            parts.append(value.reshape(2, 64, 128))
        for kind in range(2):
            slot = 2 * g + kind
            value = jnp.concatenate([parts[0][kind], parts[1][kind]], axis=0)
            o = DISTANCES[g][kind]
            if o == 0:
                total[...] = value
                continue
            encode(value, z_out.at[slot])
            copy = remote(z_out.at[slot], z_in.at[o], z_send.at[o], z_recv.at[o], even_peers[o // 2 - 1])
            copy.start()
            pending.append(copy)

    compute(0)
    for part in range(2):
        relay(part, 0)
    compute(1)
    middle(0)
    for part in range(2):
        relay(part, 1)
    last(0)
    middle(1)
    last(1)

    sums = total[...]
    for o in (4, 2, 6):
        remote(z_out.at[0], z_in.at[o], z_send.at[o], z_recv.at[o], even_peers[o // 2 - 1]).wait_recv()
        sums = sums + decode(z_in.at[o])
    encode(sums, ag_out)
    copies = []
    for o in FAR_FIRST:
        copy = remote(ag_out, ag_in.at[o], ag_send.at[o], ag_recv.at[o], ctx_peers[o - 1])
        copy.start()
        copies.append(copy)
    out_ref[ctx] = decode(ag_out).reshape(4, 32, 128)
    for copy in pending:
        copy.wait_send()
    for copy in [*kv_copies, *near_copies, *dkv_copies]:
        copy.wait_send()
    dq_copy.wait()
    for copy in copies:
        copy.wait()
    for o in range(1, 8):
        out_ref[lax.rem(ctx + 8 - o, 8)] = decode(ag_in.at[o]).reshape(4, 32, 128)


def backward(order, lens, queries, cots, keys, values, hidden):
    rows = hidden.shape[0]
    dma = pltpu.SemaphoreType.DMA
    codes = jnp.int16
    reach, width = WINDOW * SPAN, GROUP * SPAN
    hbm = pl.BlockSpec(memory_space=pl.ANY)
    smem = pl.BlockSpec(memory_space=pltpu.SMEM)
    return pl.pallas_call(
        backward_kernel,
        out_shape=[
            jax.ShapeDtypeStruct(queries.shape, BF16),
            jax.ShapeDtypeStruct((8, 4, 32, 128), F32),
        ],
        in_specs=[smem, smem, hbm, hbm, hbm, hbm, hbm],
        out_specs=[hbm, pl.BlockSpec(memory_space=pltpu.VMEM)],
        scratch_shapes=[
            pltpu.VMEM(queries.shape, BF16),
            pltpu.VMEM(queries.shape, BF16),
            pltpu.VMEM((8 * rows, HEAD), BF16),
            pltpu.VMEM((8 * rows, HEAD), BF16),
            pltpu.VMEM((2, reach, HEAD), BF16),
            pltpu.VMEM((2, reach, HEAD), BF16),
            pltpu.VMEM((2, HEAD, reach), BF16),
            pltpu.VMEM((2, reach, width), F32),
            pltpu.VMEM((32 // GROUP, reach, width), F32),
            pltpu.VMEM((32 // GROUP, 8, width), F32),
            pltpu.VMEM((reach, width), F32),
            pltpu.VMEM((reach, width), BF16),
            pltpu.VMEM((32 // GROUP, reach, width), BF16),
            pltpu.VMEM((2, reach, HEAD), F32),
            pltpu.VMEM((2, reach, HEAD), F32),
            pltpu.VMEM((8, rows + 16, HEAD), codes),
            pltpu.VMEM((8, rows + 16, HEAD), codes),
            pltpu.VMEM((8, rows + 16, HEAD), codes),
            pltpu.VMEM((8, rows + 16, HEAD), codes),
            pltpu.VMEM(queries.shape, BF16),
            dma((5,)), dma((2, 8)), dma((2, 8)), dma((8,)), dma((8,)), dma((8,)), dma((8,)),
            pltpu.VMEM((8, 4 * rows, 512), BF16),
            pltpu.VMEM((6 * rows, 256), BF16),
            pltpu.VMEM((256, 6 * rows), BF16),
            pltpu.VMEM((2, NGROUPS, 4, 8, 2, 32, 128), F32),
            pltpu.VMEM((2, NGROUPS, 6, 272, 128), codes),
            pltpu.VMEM((2, NGROUPS, 6, 272, 128), codes),
            pltpu.VMEM((2, NGROUPS, 4, 2, 2, 32, 128), F32),
            pltpu.VMEM((2, NGROUPS, 4, 144, 128), codes),
            pltpu.VMEM((2, NGROUPS, 4, 144, 128), codes),
            pltpu.VMEM((8, 144, 128), codes),
            pltpu.VMEM((8, 144, 128), codes),
            pltpu.VMEM((128, 128), F32),
            pltpu.VMEM((144, 128), codes),
            pltpu.VMEM((8, 144, 128), codes),
            dma((8,)), dma((8,)), dma((8,)), dma((4, 4)), dma((8, 2)), dma((2, 5)), dma((2, 5)),
            dma((2, NGROUPS, 6)), dma((2, NGROUPS, 6)), dma((2, NGROUPS, 4)), dma((2, NGROUPS, 4)),
            dma((8,)), dma((8,)), dma((8,)), dma((8,)),
        ],
        compiler_params=pltpu.CompilerParams(
            collective_id=0, has_side_effects=True, vmem_limit_bytes=60 * 2**20
        ),
        name="backward",
    )(order, lens, queries, cots, keys, values, hidden)


def adam_kernel(
    dq_in, grad_t, m_codes, m_scales, v_codes, v_scales, dq, update, m_norm, m_absmax, v_norm, v_absmax, grad
):
    dq[...] = dq_in[...]
    grad[...] = grad_t[:, 0].reshape(256, 128).T
    base = pl.program_id(0) * 16
    for b in range(16):
        rows = pl.ds(b * 8, 8)
        g = grad[rows, :]
        m = 0.9 * (m_codes[rows, :].astype(F32) * (m_scales[base + b] * (1.0 / 127.0))) + 0.1 * g
        v = 0.95 * (v_codes[rows, :].astype(F32) * (v_scales[base + b] * (1.0 / 255.0))) + 0.05 * g * g
        update[rows, :] = m * (1.0 / (1.0 - 0.9**STEP)) / (jnp.sqrt(v * (1.0 / (1.0 - 0.95**STEP))) + 1e-08)
        m_top = jnp.max(jnp.abs(m))
        v_top = jnp.max(v)
        m_absmax[base + b] = m_top
        v_absmax[base + b] = v_top
        m_norm[rows, :] = m / (m_top + 1e-06)
        v_norm[rows, :] = v / (v_top + 1e-06)


def adam(dq, grad_t, m_codes, m_scales, v_codes, v_scales):
    smem = pl.BlockSpec(memory_space=pltpu.SMEM)
    rows = pl.BlockSpec((128, 256), lambda q: (q, 0))
    slab = pl.BlockSpec((dq.shape[0] // 4, dq.shape[1]), lambda q: (q, 0))
    big = jax.ShapeDtypeStruct(m_codes.shape, F32)
    small = jax.ShapeDtypeStruct(m_scales.shape, F32)
    return pl.pallas_call(
        adam_kernel,
        grid=(4,),
        out_shape=[jax.ShapeDtypeStruct(dq.shape, dq.dtype), big, big, small, big, small],
        in_specs=[slab, pl.BlockSpec((8, 1, 32, 128), lambda q: (0, q, 0, 0)), rows, smem, rows, smem],
        out_specs=[slab, rows, rows, smem, rows, smem],
        scratch_shapes=[pltpu.VMEM((128, 256), F32)],
        compiler_params=pltpu.CompilerParams(vmem_limit_bytes=60 * 2**20),
        name="adam",
    )(dq, grad_t, m_codes, m_scales, v_codes, v_scales)


def shards(
    q_heads, keys, values, out_grad, hidden_in, doc_lengths, span_order, m_codes, m_scales, v_codes, v_scales
):
    dq, grad_t = backward(
        span_order, doc_lengths, q_heads[0], out_grad[0], keys[0], values[0], hidden_in[0]
    )
    dq, update, m_norm, m_absmax, v_norm, v_absmax = adam(dq, grad_t, m_codes, m_scales, v_codes, v_scales)
    return (dq[None], update, m_norm, m_absmax, v_norm, v_absmax)


def solution(mesh):
    in_specs = (
        P("dp", "ctx", None),
        P("dp", "ctx", None),
        P("dp", "ctx", None),
        P("dp", "ctx", None),
        P("dp", "ctx", None),
        P("dp", None),
        P(),
        P("dp", None),
        P("dp"),
        P("dp", None),
        P("dp"),
    )
    out_specs = (
        P("dp", "ctx", None),
        P("dp", None),
        P("dp", None),
        P("dp"),
        P("dp", None),
        P("dp"),
    )
    return jax.shard_map(shards, mesh=mesh, in_specs=in_specs, out_specs=out_specs, check_vma=False)
```

```python
import functools
import math

import jax
import jax.numpy as jnp
from jax import lax
from jax.experimental import pallas as pl
from jax.experimental.pallas import tpu as pltpu
from jax.sharding import PartitionSpec as P

STEP = 10
SPAN = 96
WINDOW = 7
HEAD = 128
GROUP = 8
EARLY = 12
NGROUPS = 2
FAR_FIRST = (4, 3, 5, 2, 6, 1, 7)
DISTANCES = ((4, 2), (0, 6))
F32 = jnp.float32
BF16 = jnp.bfloat16
MESH = pl.DeviceIdType.MESH


def remote(src, dst, send, recv, device):
    return pltpu.make_async_remote_copy(
        src_ref=src, dst_ref=dst, send_sem=send, recv_sem=recv, device_id=device, device_id_type=MESH
    )


def greet(devices):
    barrier = pltpu.get_barrier_semaphore()
    for device in devices:
        pl.semaphore_signal(barrier, inc=1, device_id=device, device_id_type=MESH)
    pl.semaphore_wait(barrier, len(devices))


def encode(values, message):
    rows = values.shape[0]
    top = jnp.max(jnp.abs(values), axis=0, keepdims=True)
    power = jnp.ceil(jnp.log2(jnp.maximum(top, 1e-30)))
    codes = jnp.round(values * (jnp.exp2(-power) * 32000.0))
    message[pl.ds(0, rows), :] = codes.astype(jnp.int32).astype(jnp.int16)
    head = jnp.broadcast_to(power, (16, values.shape[1]))
    message[pl.ds(rows, 16), :] = head.astype(jnp.int32).astype(jnp.int16)


def decode(message):
    rows = message.shape[0] - 16
    power = message[pl.ds(rows, 16), :].astype(jnp.int32).astype(F32)[0:1, :]
    codes = message[pl.ds(0, rows), :].astype(jnp.int32).astype(F32)
    return codes * (jnp.exp2(power) * (1.0 / 32000.0))


def dot_t(left, right):
    return lax.dot_general(left, right, (((1,), (1,)), ((), ())), preferred_element_type=F32)


def window_of(order, place, stored, window):
    def pick(r, carry):
        wanted = place - (WINDOW - 1) + r
        block = jnp.zeros((SPAN, HEAD), BF16)
        for s in range(16):
            weight = jnp.where(order[s] == wanted, 1.0, 0.0).astype(BF16)
            block = block + stored[pl.ds(s * SPAN, SPAN), :] * weight
        window[pl.ds(pl.multiple_of(r * SPAN, SPAN), SPAN), :] = block
        return carry

    lax.fori_loop(0, WINDOW, pick, 0)


def mask_bias(place, lens, bias):
    width = GROUP * SPAN
    lane = lax.broadcasted_iota(jnp.int32, (1, width), 1)
    head = jnp.zeros_like(lane)
    for h in range(1, GROUP):
        head = head + (lane >= h * SPAN).astype(jnp.int32)
    query_pos = place * SPAN + lane - head * SPAN
    begin = jnp.zeros_like(lane)
    end = jnp.int32(0)
    for k in range(8):
        end = end + lens[0, k]
        begin = jnp.where(query_pos >= end, end, begin)
    for r in range(WINDOW):
        key_pos = (place - (WINDOW - 1) + r) * SPAN + lax.broadcasted_iota(jnp.int32, (SPAN, width), 0)
        allowed = (key_pos <= query_pos) & (key_pos >= begin)
        bias[pl.ds(r * SPAN, SPAN), :] = jnp.where(allowed, 0.0, -1e30)


def heads_of(ref, qb, grp):
    rows = pl.ds(pl.multiple_of(qb * SPAN, SPAN), SPAN)
    wide = GROUP * HEAD
    lanes = [pl.ds(pl.multiple_of(grp * wide, wide) + h * HEAD, HEAD) for h in range(GROUP)]
    return rows, lanes, jnp.concatenate([ref[rows, c] for c in lanes], axis=0)


def softmax_numerators(k7, queries, bias, expo_scr, inv_scr):
    factor = math.log2(math.e) / math.sqrt(HEAD)
    width = GROUP * SPAN
    parts = [pl.ds(r * SPAN, SPAN) for r in range(WINDOW)]
    expo_scr[...] = dot_t(k7[...], queries)
    top = jnp.full((8, width), -3e38, F32)
    for part in parts:
        scores = expo_scr[part, :] + bias[part, :]
        expo_scr[part, :] = scores
        top = jnp.maximum(top, jnp.max(scores.reshape(SPAN // 8, 8, width), axis=0))
    top = jnp.max(top, axis=0, keepdims=True)
    denom = jnp.zeros((8, width), F32)
    for part in parts:
        expo = jnp.exp2((expo_scr[part, :] - top) * factor)
        expo_scr[part, :] = expo
        denom = denom + jnp.sum(expo.reshape(SPAN // 8, 8, width), axis=0)
    inv_scr[...] = jnp.broadcast_to(1.0 / jnp.sum(denom, axis=0, keepdims=True), (8, width))


def softmax_terms(v7, cots, expo_scr, inv_scr, d_scr, p_scr, ds_scr):
    width = GROUP * SPAN
    parts = [pl.ds(r * SPAN, SPAN) for r in range(WINDOW)]
    d_scr[...] = dot_t(v7[...], cots)
    inv = inv_scr[0:1, :]
    weighted = jnp.zeros((8, width), F32)
    for part in parts:
        prob = expo_scr[part, :] * inv
        expo_scr[part, :] = prob
        p_scr[part, :] = prob.astype(BF16)
        weighted = weighted + jnp.sum((prob * d_scr[part, :]).reshape(SPAN // 8, 8, width), axis=0)
    delta = jnp.sum(weighted, axis=0, keepdims=True)
    for part in parts:
        ds_scr[part, :] = (expo_scr[part, :] * (d_scr[part, :] - delta)).astype(BF16)


def messages(order, places, found, out, gain):
    def write(c, carry):
        halves = []
        for half in range(2):
            place = order[2 * c + half]
            value = jnp.zeros((SPAN, HEAD), F32)
            for qb in range(2):
                for r in range(WINDOW):
                    weight = jnp.where(place - (places[qb] - (WINDOW - 1)) == r, 1.0, 0.0)
                    value = value + found[qb, pl.ds(r * SPAN, SPAN), :] * weight
            halves.append(value)
        encode(jnp.concatenate(halves, axis=0) * gain, out.at[c])
        return carry

    lax.fori_loop(0, 8, write, 0)


def backward_kernel(
    order, lens, q_hbm, g_hbm, k_hbm, v_hbm, hid, dq_hbm, out_ref,
    q_ref, g_ref, kall, vall, k7, v7, k7t, bias, expo_all, inv_all, d_scr, p_scr, ds_all, dkw, dvw, dk_out, dv_out, dk_in, dv_in, dq_ref,
    load_sem, kv_send, kv_recv, dk_send, dk_recv, dv_send, dv_recv,
    held, dkv2, dkvt, first, out1, in1, second, out2, in2, z_out, z_in, total, ag_out, ag_in,
    hid_own, hid_send, hid_recv, near_send, near_recv, pair_send, pair_recv,
    send1, recv1, send2, recv2, z_send, z_recv, ag_send, ag_recv,
):
    dp, ctx = lax.axis_index("dp"), lax.axis_index("ctx")
    x, ylo = ctx // 2, lax.rem(ctx, 2)
    z, yhi, core = dp // 4, lax.rem(dp // 2, 2), lax.rem(dp, 2)
    y = yhi * 2 + ylo
    rows = hid.shape[0]

    def at(xx, yy, zz):
        return (zz * 4 + (yy // 2) * 2 + core, xx * 2 + lax.rem(yy, 2))

    x_ring = (x, *[at(lax.rem(x + k, 4), y, z) for k in range(1, 4)])
    y_ring = (y, *[at(x, lax.rem(y + k, 4), z) for k in range(1, 4)])
    pair = (dp + 1 - 2 * core, ctx)
    ctx_peers = [(dp, lax.rem(ctx + o, 8)) for o in range(1, 8)]
    even_peers = [at(x, y, lax.rem(z + o, 8)) for o in (2, 4, 6)]
    y_far = at(x, lax.rem(y + 2, 4), z)
    across = at(x, lax.rem(y + 3 + 2 * ylo, 4), z)

    def columns(zz, kind, j, yh, c):
        distance = 4 - 4 * j + kind * (8 * j - 2)
        block = lax.rem(zz + distance, 8) * 4 + yh * 2 + c
        return pl.ds(pl.multiple_of(block * 512, 512), 512)

    parity = lax.rem(z, 2)
    wanted = lax.rem(z, 4) // 2
    near = []
    for n in range(2):
        zz = lax.rem(z + (1 - 2 * n) * (1 - 2 * parity) + 8, 8)
        for c in range(2):
            near.append((zz, lax.rem(core + c, 2)))
    sharers = [(zz * 4 + yhi * 2 + cc, ctx) for zz, cc in near]

    mine = pl.ds(pl.multiple_of(ctx * rows, rows), rows)
    loads = [
        pltpu.make_async_copy(src, dst, load_sem.at[k])
        for k, (src, dst) in enumerate(
            ((k_hbm, kall.at[mine]), (v_hbm, vall.at[mine]), (q_hbm, q_ref), (g_hbm, g_ref))
        )
    ]
    for copy in loads:
        copy.start()
    greet([*ctx_peers, *even_peers, *sharers, pair, across, y_far])
    kv_copies = []
    for which, (src, dst) in enumerate(((k_hbm, kall), (v_hbm, vall))):
        for o in FAR_FIRST:
            copy = remote(src, dst.at[mine], kv_send.at[which, o], kv_recv.at[which, o], ctx_peers[o - 1])
            copy.start()
            kv_copies.append(copy)
    near_copies = []
    for j in range(2):
        for yh in range(2):
            for n, (zz, cc) in enumerate(near):
                slot, block = j * 4 + wanted * 2 + yh, 2 + n % 2
                copy = remote(
                    hid.at[:, columns(zz, wanted, j, yh, cc)],
                    held.at[slot, pl.ds(block * rows, rows)],
                    near_send.at[j * 2 + yh, n],
                    near_recv.at[slot, n % 2],
                    sharers[n],
                )
                near_copies.append(copy)
                if len(near_copies) <= EARLY:
                    copy.start()
    own, swaps = [], []
    for slot in range(8):
        j, kind, yh = slot // 4, slot // 2 % 2, slot % 2
        own.append(
            pltpu.make_async_copy(
                hid.at[:, columns(z, kind, j, yh, core)], held.at[slot, pl.ds(0, rows)], hid_own.at[slot]
            )
        )
        own[slot].start()
        copy = remote(
            hid.at[:, columns(z, kind, j, yh, 1 - core)],
            held.at[slot, pl.ds(rows, rows)],
            hid_send.at[slot],
            hid_recv.at[slot],
            pair,
        )
        copy.start()
        swaps.append(copy)

    places = [order[2 * ctx], order[2 * ctx + 1]]
    for qb in range(2):
        mask_bias(places[qb], lens, bias.at[qb])
    dvw[...] = jnp.zeros_like(dvw)
    dkw[...] = jnp.zeros_like(dkw)
    def all_here(which, src, dst):
        loads[which].wait()
        for o in FAR_FIRST:
            theirs = pl.ds(pl.multiple_of(lax.rem(ctx + 8 - o, 8) * rows, rows), rows)
            remote(src, dst.at[theirs], kv_send.at[which, o], kv_recv.at[which, o], ctx_peers[o - 1]).wait_recv()

    reach = pl.ds(0, WINDOW * SPAN)
    steps = 2 * 16 // GROUP
    scale = 1.0 / math.sqrt(HEAD)
    all_here(0, k_hbm, kall)
    loads[2].wait()
    for qb in range(2):
        window_of(order, places[qb], kall, k7.at[qb])

    def numerator_step(it, carry):
        qb, grp = it // (steps // 2), lax.rem(it, steps // 2)
        queries = heads_of(q_ref, qb, grp)[2]
        softmax_numerators(k7.at[qb], queries, bias.at[qb], expo_all.at[it], inv_all.at[it])
        return carry

    lax.fori_loop(0, steps, numerator_step, 0)
    all_here(1, v_hbm, vall)
    loads[3].wait()
    for qb in range(2):
        window_of(order, places[qb], vall, v7.at[qb])

    def score_step(it, carry):
        qb, grp = it // (steps // 2), lax.rem(it, steps // 2)
        cots = heads_of(g_ref, qb, grp)[2]
        softmax_terms(v7.at[qb], cots, expo_all.at[it], inv_all.at[it], d_scr, p_scr, ds_all.at[it])
        dvw[qb, reach, :] += jnp.dot(p_scr[...], cots, preferred_element_type=F32)
        return carry

    lax.fori_loop(0, steps, score_step, 0)

    def exchange(out, into, send, recv):
        copies = []
        for o in FAR_FIRST:
            copy = remote(out.at[lax.rem(ctx + o, 8)], into.at[o], send.at[o], recv.at[o], ctx_peers[o - 1])
            copy.start()
            copies.append(copy)
        return copies

    messages(order, places, dvw, dv_out, 1.0)
    dv_copies = exchange(dv_out, dv_in, dv_send, dv_recv)

    def key_step(it, carry):
        qb, grp = it // (steps // 2), lax.rem(it, steps // 2)
        queries = heads_of(q_ref, qb, grp)[2]
        dkw[qb, reach, :] += jnp.dot(ds_all[it], queries, preferred_element_type=F32)
        return carry

    lax.fori_loop(0, steps, key_step, 0)
    messages(order, places, dkw, dk_out, scale)
    dk_copies = exchange(dk_out, dk_in, dk_send, dk_recv)

    for qb in range(2):
        k7t[qb] = k7[qb].astype(F32).T.astype(BF16)

    def query_step(it, carry):
        qb, grp = it // (steps // 2), lax.rem(it, steps // 2)
        query_rows, lanes, _ = heads_of(q_ref, qb, grp)
        dq = (jnp.dot(k7t[qb], ds_all[it], preferred_element_type=F32) * scale).T.astype(BF16)
        for h in range(GROUP):
            dq_ref[query_rows, lanes[h]] = dq[h * SPAN : (h + 1) * SPAN, :]
        return carry

    lax.fori_loop(0, steps, query_step, 0)
    dq_copy = pltpu.make_async_copy(dq_ref, dq_hbm, load_sem.at[4])
    dq_copy.start()

    dkv_copies = []
    for side, (copies, out, into) in enumerate(((dk_copies, dk_out, dk_in), (dv_copies, dv_out, dv_in))[::-1]):
        for copy in copies:
            copy.wait()
        value = decode(out.at[ctx])
        for o in range(1, 8):
            value = value + decode(into.at[o])
        lanes = pl.ds((1 - side) * HEAD, HEAD)
        dkv2[pl.ds(0, rows), lanes] = value.astype(BF16)
        for n, device in enumerate([pair, *sharers]):
            start, arrival = rows, 0
            if n:
                arrival = 1 + 2 * wanted + (n - 1) % 2
                start = (1 + arrival) * rows
            copy = remote(
                dkv2.at[pl.ds(0, rows), lanes],
                dkv2.at[pl.ds(pl.multiple_of(start, rows), rows), lanes],
                pair_send.at[side, n],
                pair_recv.at[side, arrival],
                device,
            )
            copy.start()
            dkv_copies.append(copy)
    for copy in near_copies[EARLY:]:
        copy.start()
    for side in range(2):
        for n in range(5):
            lanes = pl.ds((1 - side) * HEAD, HEAD)
            remote(
                dkv2.at[pl.ds(0, rows), lanes],
                dkv2.at[pl.ds((1 + n) * rows, rows), lanes],
                pair_send.at[side, n],
                pair_recv.at[side, n],
                pair,
            ).wait_recv()
    dkvt[...] = dkv2[...].astype(F32).T.astype(BF16)

    rings = ((x_ring, y_ring), (y_ring, x_ring))
    pending = []

    def flat(value):
        return value.reshape(-1, 128)

    def piece(part, g, place, high):
        return flat(first[part, g, place, pl.ds(4 * high, 4)])

    def copy_of(part, g, k):
        device = rings[part][0][1 if k % 2 == 0 else 3]
        return remote(out1.at[part, g, k], in1.at[part, g, k], send1.at[part, g, k], recv1.at[part, g, k], device)

    def post(part, g, k, value):
        encode(value, out1.at[part, g, k])
        copy = copy_of(part, g, k)
        copy.start()
        pending.append(copy)

    def arrived(part, g, k):
        copy_of(part, g, k).wait_recv()
        return decode(in1.at[part, g, k])

    def begin(part, g):
        place = rings[part][0][0]
        after, before, opposite = lax.rem(place + 1, 4), lax.rem(place + 3, 4), lax.rem(place + 2, 4)
        for k, (owner, high) in enumerate(((opposite, 0), (opposite, 1), (after, 1), (before, 0))):
            post(part, g, k, piece(part, g, owner, high))

    def relay(part, g):
        place = rings[part][0][0]
        after, before = lax.rem(place + 1, 4), lax.rem(place + 3, 4)
        for k, (owner, high) in enumerate(((after, 0), (before, 1))):
            post(part, g, 4 + k, arrived(part, g, k) + piece(part, g, owner, high))

    def finish(part, g):
        place = rings[part][0][0]
        low = arrived(part, g, 3) + arrived(part, g, 4) + piece(part, g, place, 0)
        high = arrived(part, g, 2) + arrived(part, g, 5) + piece(part, g, place, 1)
        return low, high

    def direct(part, g, k):
        return remote(
            out2.at[part, g, k], in2.at[part, g, k], send2.at[part, g, k], recv2.at[part, g, k], rings[part][1][k]
        )

    def compute(g):
        for slot in range(4 * g, 4 * g + 4):
            own[slot].wait()
            swaps[slot].wait()
            for c in range(2):
                block = pl.ds((2 + c) * rows, rows)
                remote(
                    hid.at[:, pl.ds(0, 512)], held.at[slot, block], near_send.at[0, 0], near_recv.at[slot, c], pair
                ).wait_recv()

        def block(k, carry):
            kind, yh = k // 2, lax.rem(k, 2)
            theirs = pl.ds(pl.multiple_of(2 * rows * (1 + kind), 128), 2 * rows)
            here, both = pl.ds(0, 2 * rows), pl.ds(2 * rows, 2 * rows)
            product = jnp.dot(dkvt[:, 0 : 2 * rows], held[4 * g + k, here], preferred_element_type=F32)
            product = product + jnp.dot(
                dkvt[:, theirs], held[4 * g + k, both], preferred_element_type=F32
            )
            for xx in range(4):
                for yl in range(2):
                    r0 = (xx * 2 + yl) * 32
                    yy = yh * 2 + yl
                    for side in range(2):
                        first[0, g, xx, yy * 2 + kind, side] = product[r0 : r0 + 32, side * 128 : side * 128 + 128]
                        first[1, g, yy, xx * 2 + kind, side] = product[r0 : r0 + 32, side * 128 + 256 : side * 128 + 384]
            return carry

        lax.fori_loop(0, 4, block, 0)
        for part in range(2):
            begin(part, g)

    def middle(g):
        for part in range(2):
            low, high = finish(part, g)
            for t in range(4):
                half = (low, high)[t // 2].reshape(2, 2, 2, 32, 128)
                second[part, g, t] = half[t % 2]
            place = rings[part][1][0]
            for k in (2, 1, 3):
                encode(flat(second[part, g, lax.rem(place + k, 4)]), out2.at[part, g, k])
                copy = direct(part, g, k)
                copy.start()
                pending.append(copy)

    def last(g):
        parts = []
        for part in range(2):
            value = flat(second[part, g, rings[part][1][0]])
            for k in (1, 3, 2):
                direct(part, g, k).wait_recv()
                value = value + decode(in2.at[part, g, k])
            parts.append(value.reshape(2, 64, 128))
        for kind in range(2):
            slot = 2 * g + kind
            value = jnp.concatenate([parts[0][kind], parts[1][kind]], axis=0)
            o = DISTANCES[g][kind]
            if o == 0:
                total[...] = value
                continue
            encode(value, z_out.at[slot])
            copy = remote(z_out.at[slot], z_in.at[o], z_send.at[o], z_recv.at[o], even_peers[o // 2 - 1])
            copy.start()
            pending.append(copy)

    compute(0)
    for part in range(2):
        relay(part, 0)
    compute(1)
    middle(0)
    for part in range(2):
        relay(part, 1)
    last(0)
    middle(1)
    last(1)

    sums = total[...]
    for o in (4, 2, 6):
        remote(z_out.at[0], z_in.at[o], z_send.at[o], z_recv.at[o], even_peers[o // 2 - 1]).wait_recv()
        sums = sums + decode(z_in.at[o])
    encode(sums, ag_out)
    copies = []
    for o in FAR_FIRST:
        copy = remote(ag_out, ag_in.at[o], ag_send.at[o], ag_recv.at[o], ctx_peers[o - 1])
        copy.start()
        copies.append(copy)
    out_ref[ctx] = decode(ag_out).reshape(4, 32, 128)
    for copy in pending:
        copy.wait_send()
    for copy in [*kv_copies, *near_copies, *dkv_copies]:
        copy.wait_send()
    dq_copy.wait()
    for copy in copies:
        copy.wait()
    for o in range(1, 8):
        out_ref[lax.rem(ctx + 8 - o, 8)] = decode(ag_in.at[o]).reshape(4, 32, 128)


def backward(order, lens, queries, cots, keys, values, hidden):
    rows = hidden.shape[0]
    dma = pltpu.SemaphoreType.DMA
    codes = jnp.int16
    reach, width = WINDOW * SPAN, GROUP * SPAN
    hbm = pl.BlockSpec(memory_space=pl.ANY)
    smem = pl.BlockSpec(memory_space=pltpu.SMEM)
    return pl.pallas_call(
        backward_kernel,
        out_shape=[
            jax.ShapeDtypeStruct(queries.shape, BF16),
            jax.ShapeDtypeStruct((8, 4, 32, 128), F32),
        ],
        in_specs=[smem, smem, hbm, hbm, hbm, hbm, hbm],
        out_specs=[hbm, pl.BlockSpec(memory_space=pltpu.VMEM)],
        scratch_shapes=[
            pltpu.VMEM(queries.shape, BF16),
            pltpu.VMEM(queries.shape, BF16),
            pltpu.VMEM((8 * rows, HEAD), BF16),
            pltpu.VMEM((8 * rows, HEAD), BF16),
            pltpu.VMEM((2, reach, HEAD), BF16),
            pltpu.VMEM((2, reach, HEAD), BF16),
            pltpu.VMEM((2, HEAD, reach), BF16),
            pltpu.VMEM((2, reach, width), F32),
            pltpu.VMEM((32 // GROUP, reach, width), F32),
            pltpu.VMEM((32 // GROUP, 8, width), F32),
            pltpu.VMEM((reach, width), F32),
            pltpu.VMEM((reach, width), BF16),
            pltpu.VMEM((32 // GROUP, reach, width), BF16),
            pltpu.VMEM((2, reach, HEAD), F32),
            pltpu.VMEM((2, reach, HEAD), F32),
            pltpu.VMEM((8, rows + 16, HEAD), codes),
            pltpu.VMEM((8, rows + 16, HEAD), codes),
            pltpu.VMEM((8, rows + 16, HEAD), codes),
            pltpu.VMEM((8, rows + 16, HEAD), codes),
            pltpu.VMEM(queries.shape, BF16),
            dma((5,)), dma((2, 8)), dma((2, 8)), dma((8,)), dma((8,)), dma((8,)), dma((8,)),
            pltpu.VMEM((8, 4 * rows, 512), BF16),
            pltpu.VMEM((6 * rows, 256), BF16),
            pltpu.VMEM((256, 6 * rows), BF16),
            pltpu.VMEM((2, NGROUPS, 4, 8, 2, 32, 128), F32),
            pltpu.VMEM((2, NGROUPS, 6, 272, 128), codes),
            pltpu.VMEM((2, NGROUPS, 6, 272, 128), codes),
            pltpu.VMEM((2, NGROUPS, 4, 2, 2, 32, 128), F32),
            pltpu.VMEM((2, NGROUPS, 4, 144, 128), codes),
            pltpu.VMEM((2, NGROUPS, 4, 144, 128), codes),
            pltpu.VMEM((8, 144, 128), codes),
            pltpu.VMEM((8, 144, 128), codes),
            pltpu.VMEM((128, 128), F32),
            pltpu.VMEM((144, 128), codes),
            pltpu.VMEM((8, 144, 128), codes),
            dma((8,)), dma((8,)), dma((8,)), dma((4, 4)), dma((8, 2)), dma((2, 5)), dma((2, 5)),
            dma((2, NGROUPS, 6)), dma((2, NGROUPS, 6)), dma((2, NGROUPS, 4)), dma((2, NGROUPS, 4)),
            dma((8,)), dma((8,)), dma((8,)), dma((8,)),
        ],
        compiler_params=pltpu.CompilerParams(
            collective_id=0, has_side_effects=True, vmem_limit_bytes=60 * 2**20
        ),
        name="backward",
    )(order, lens, queries, cots, keys, values, hidden)


def adam_kernel(
    dq_in, grad_t, m_codes, m_scales, v_codes, v_scales, dq, update, m_norm, m_absmax, v_norm, v_absmax, grad
):
    dq[...] = dq_in[...]
    grad[...] = grad_t[:, 0].reshape(256, 128).T
    base = pl.program_id(0) * 16
    for b in range(16):
        rows = pl.ds(b * 8, 8)
        g = grad[rows, :]
        m = 0.9 * (m_codes[rows, :].astype(F32) * (m_scales[base + b] * (1.0 / 127.0))) + 0.1 * g
        v = 0.95 * (v_codes[rows, :].astype(F32) * (v_scales[base + b] * (1.0 / 255.0))) + 0.05 * g * g
        update[rows, :] = m * (1.0 / (1.0 - 0.9**STEP)) / (jnp.sqrt(v * (1.0 / (1.0 - 0.95**STEP))) + 1e-08)
        m_top = jnp.max(jnp.abs(m))
        v_top = jnp.max(v)
        m_absmax[base + b] = m_top
        v_absmax[base + b] = v_top
        m_norm[rows, :] = m / (m_top + 1e-06)
        v_norm[rows, :] = v / (v_top + 1e-06)


def adam(dq, grad_t, m_codes, m_scales, v_codes, v_scales):
    smem = pl.BlockSpec(memory_space=pltpu.SMEM)
    rows = pl.BlockSpec((128, 256), lambda q: (q, 0))
    slab = pl.BlockSpec((dq.shape[0] // 4, dq.shape[1]), lambda q: (q, 0))
    big = jax.ShapeDtypeStruct(m_codes.shape, F32)
    small = jax.ShapeDtypeStruct(m_scales.shape, F32)
    return pl.pallas_call(
        adam_kernel,
        grid=(4,),
        out_shape=[jax.ShapeDtypeStruct(dq.shape, dq.dtype), big, big, small, big, small],
        in_specs=[slab, pl.BlockSpec((8, 1, 32, 128), lambda q: (0, q, 0, 0)), rows, smem, rows, smem],
        out_specs=[slab, rows, rows, smem, rows, smem],
        scratch_shapes=[pltpu.VMEM((128, 256), F32)],
        compiler_params=pltpu.CompilerParams(vmem_limit_bytes=60 * 2**20),
        name="adam",
    )(dq, grad_t, m_codes, m_scales, v_codes, v_scales)


def shards(
    q_heads, keys, values, out_grad, hidden_in, doc_lengths, span_order, m_codes, m_scales, v_codes, v_scales
):
    dq, grad_t = backward(
        span_order, doc_lengths, q_heads[0], out_grad[0], keys[0], values[0], hidden_in[0]
    )
    dq, update, m_norm, m_absmax, v_norm, v_absmax = adam(dq, grad_t, m_codes, m_scales, v_codes, v_scales)
    return (dq[None], update, m_norm, m_absmax, v_norm, v_absmax)


def solution(mesh):
    in_specs = (
        P("dp", "ctx", None),
        P("dp", "ctx", None),
        P("dp", "ctx", None),
        P("dp", "ctx", None),
        P("dp", "ctx", None),
        P("dp", None),
        P(),
        P("dp", None),
        P("dp"),
        P("dp", None),
        P("dp"),
    )
    out_specs = (
        P("dp", "ctx", None),
        P("dp", None),
        P("dp", None),
        P("dp"),
        P("dp", None),
        P("dp"),
    )
    return jax.shard_map(shards, mesh=mesh, in_specs=in_specs, out_specs=out_specs, check_vma=False)
```

```python
import functools
import math

import jax
import jax.numpy as jnp
from jax import lax
from jax.experimental import pallas as pl
from jax.experimental.pallas import tpu as pltpu
from jax.sharding import PartitionSpec as P

STEP = 10
SPAN = 96
WINDOW = 7
HEAD = 128
GROUP = 8
EARLY = 12
NGROUPS = 2
FAR_FIRST = (4, 3, 5, 2, 6, 1, 7)
DISTANCES = ((4, 2), (0, 6))
F32 = jnp.float32
BF16 = jnp.bfloat16
MESH = pl.DeviceIdType.MESH


def remote(src, dst, send, recv, device):
    return pltpu.make_async_remote_copy(
        src_ref=src, dst_ref=dst, send_sem=send, recv_sem=recv, device_id=device, device_id_type=MESH
    )


def greet(devices):
    barrier = pltpu.get_barrier_semaphore()
    for device in devices:
        pl.semaphore_signal(barrier, inc=1, device_id=device, device_id_type=MESH)
    pl.semaphore_wait(barrier, len(devices))


def encode(values, message):
    rows = values.shape[0]
    top = jnp.max(jnp.abs(values), axis=0, keepdims=True)
    power = jnp.ceil(jnp.log2(jnp.maximum(top, 1e-30)))
    codes = jnp.round(values * (jnp.exp2(-power) * 32000.0))
    message[pl.ds(0, rows), :] = codes.astype(jnp.int32).astype(jnp.int16)
    head = jnp.broadcast_to(power, (16, values.shape[1]))
    message[pl.ds(rows, 16), :] = head.astype(jnp.int32).astype(jnp.int16)


def decode(message):
    rows = message.shape[0] - 16
    power = message[pl.ds(rows, 16), :].astype(jnp.int32).astype(F32)[0:1, :]
    codes = message[pl.ds(0, rows), :].astype(jnp.int32).astype(F32)
    return codes * (jnp.exp2(power) * (1.0 / 32000.0))


def dot_t(left, right):
    return lax.dot_general(left, right, (((1,), (1,)), ((), ())), preferred_element_type=F32)


def window_of(order, place, stored, window):
    def pick(r, carry):
        wanted = place - (WINDOW - 1) + r
        block = jnp.zeros((SPAN, HEAD), BF16)
        for s in range(16):
            weight = jnp.where(order[s] == wanted, 1.0, 0.0).astype(BF16)
            block = block + stored[pl.ds(s * SPAN, SPAN), :] * weight
        window[pl.ds(pl.multiple_of(r * SPAN, SPAN), SPAN), :] = block
        return carry

    lax.fori_loop(0, WINDOW, pick, 0)


def mask_bias(place, lens, bias):
    width = GROUP * SPAN
    lane = lax.broadcasted_iota(jnp.int32, (1, width), 1)
    head = jnp.zeros_like(lane)
    for h in range(1, GROUP):
        head = head + (lane >= h * SPAN).astype(jnp.int32)
    query_pos = place * SPAN + lane - head * SPAN
    begin = jnp.zeros_like(lane)
    end = jnp.int32(0)
    for k in range(8):
        end = end + lens[0, k]
        begin = jnp.where(query_pos >= end, end, begin)
    for r in range(WINDOW):
        key_pos = (place - (WINDOW - 1) + r) * SPAN + lax.broadcasted_iota(jnp.int32, (SPAN, width), 0)
        allowed = (key_pos <= query_pos) & (key_pos >= begin)
        bias[pl.ds(r * SPAN, SPAN), :] = jnp.where(allowed, 0.0, -1e30)


def heads_of(ref, qb, grp):
    rows = pl.ds(pl.multiple_of(qb * SPAN, SPAN), SPAN)
    wide = GROUP * HEAD
    lanes = [pl.ds(pl.multiple_of(grp * wide, wide) + h * HEAD, HEAD) for h in range(GROUP)]
    return rows, lanes, jnp.concatenate([ref[rows, c] for c in lanes], axis=0)


def softmax_numerators(k7, queries, bias, expo_scr, inv_scr):
    factor = math.log2(math.e) / math.sqrt(HEAD)
    width = GROUP * SPAN
    parts = [pl.ds(r * SPAN, SPAN) for r in range(WINDOW)]
    expo_scr[...] = dot_t(k7[...], queries)
    top = jnp.full((8, width), -3e38, F32)
    for part in parts:
        scores = expo_scr[part, :] + bias[part, :]
        expo_scr[part, :] = scores
        top = jnp.maximum(top, jnp.max(scores.reshape(SPAN // 8, 8, width), axis=0))
    top = jnp.max(top, axis=0, keepdims=True)
    denom = jnp.zeros((8, width), F32)
    for part in parts:
        expo = jnp.exp2((expo_scr[part, :] - top) * factor)
        expo_scr[part, :] = expo
        denom = denom + jnp.sum(expo.reshape(SPAN // 8, 8, width), axis=0)
    inv_scr[...] = jnp.broadcast_to(1.0 / jnp.sum(denom, axis=0, keepdims=True), (8, width))


def softmax_terms(v7, cots, expo_scr, inv_scr, d_scr, p_scr, ds_scr):
    width = GROUP * SPAN
    parts = [pl.ds(r * SPAN, SPAN) for r in range(WINDOW)]
    d_scr[...] = dot_t(v7[...], cots)
    inv = inv_scr[0:1, :]
    weighted = jnp.zeros((8, width), F32)
    for part in parts:
        prob = expo_scr[part, :] * inv
        expo_scr[part, :] = prob
        p_scr[part, :] = prob.astype(BF16)
        weighted = weighted + jnp.sum((prob * d_scr[part, :]).reshape(SPAN // 8, 8, width), axis=0)
    delta = jnp.sum(weighted, axis=0, keepdims=True)
    for part in parts:
        ds_scr[part, :] = (expo_scr[part, :] * (d_scr[part, :] - delta)).astype(BF16)


def messages(order, places, found, out, gain):
    def write(c, carry):
        halves = []
        for half in range(2):
            place = order[2 * c + half]
            value = jnp.zeros((SPAN, HEAD), F32)
            for qb in range(2):
                for r in range(WINDOW):
                    weight = jnp.where(place - (places[qb] - (WINDOW - 1)) == r, 1.0, 0.0)
                    value = value + found[qb, pl.ds(r * SPAN, SPAN), :] * weight
            halves.append(value)
        encode(jnp.concatenate(halves, axis=0) * gain, out.at[c])
        return carry

    lax.fori_loop(0, 8, write, 0)


def backward_kernel(
    order, lens, q_hbm, g_hbm, k_hbm, v_hbm, hid, dq_hbm, out_ref,
    q_ref, g_ref, kall, vall, k7, v7, k7t, bias, expo_all, inv_all, d_scr, p_scr, ds_all, dkw, dvw, dk_out, dv_out, dk_in, dv_in, dq_ref,
    load_sem, kv_send, kv_recv, dk_send, dk_recv, dv_send, dv_recv,
    held, dkv2, dkvt, first, out1, in1, second, out2, in2, z_out, z_in, total, ag_out, ag_in,
    hid_own, hid_send, hid_recv, near_send, near_recv, pair_send, pair_recv,
    send1, recv1, send2, recv2, z_send, z_recv, ag_send, ag_recv,
):
    dp, ctx = lax.axis_index("dp"), lax.axis_index("ctx")
    x, ylo = ctx // 2, lax.rem(ctx, 2)
    z, yhi, core = dp // 4, lax.rem(dp // 2, 2), lax.rem(dp, 2)
    y = yhi * 2 + ylo
    rows = hid.shape[0]

    def at(xx, yy, zz):
        return (zz * 4 + (yy // 2) * 2 + core, xx * 2 + lax.rem(yy, 2))

    x_ring = (x, *[at(lax.rem(x + k, 4), y, z) for k in range(1, 4)])
    y_ring = (y, *[at(x, lax.rem(y + k, 4), z) for k in range(1, 4)])
    pair = (dp + 1 - 2 * core, ctx)
    ctx_peers = [(dp, lax.rem(ctx + o, 8)) for o in range(1, 8)]
    even_peers = [at(x, y, lax.rem(z + o, 8)) for o in (2, 4, 6)]
    y_far = at(x, lax.rem(y + 2, 4), z)
    across = at(x, lax.rem(y + 3 + 2 * ylo, 4), z)

    def columns(zz, kind, j, yh, c):
        distance = 4 - 4 * j + kind * (8 * j - 2)
        block = lax.rem(zz + distance, 8) * 4 + yh * 2 + c
        return pl.ds(pl.multiple_of(block * 512, 512), 512)

    parity = lax.rem(z, 2)
    wanted = lax.rem(z, 4) // 2
    near = []
    for n in range(2):
        zz = lax.rem(z + (1 - 2 * n) * (1 - 2 * parity) + 8, 8)
        for c in range(2):
            near.append((zz, lax.rem(core + c, 2)))
    sharers = [(zz * 4 + yhi * 2 + cc, ctx) for zz, cc in near]

    mine = pl.ds(pl.multiple_of(ctx * rows, rows), rows)
    loads = [
        pltpu.make_async_copy(src, dst, load_sem.at[k])
        for k, (src, dst) in enumerate(
            ((k_hbm, kall.at[mine]), (v_hbm, vall.at[mine]), (q_hbm, q_ref), (g_hbm, g_ref))
        )
    ]
    for copy in loads:
        copy.start()
    greet([*ctx_peers, *even_peers, *sharers, pair, across, y_far])
    kv_copies = []
    for which, (src, dst) in enumerate(((k_hbm, kall), (v_hbm, vall))):
        for o in FAR_FIRST:
            copy = remote(src, dst.at[mine], kv_send.at[which, o], kv_recv.at[which, o], ctx_peers[o - 1])
            copy.start()
            kv_copies.append(copy)
    near_copies = []
    for j in range(2):
        for yh in range(2):
            for n, (zz, cc) in enumerate(near):
                slot, block = j * 4 + wanted * 2 + yh, 2 + n % 2
                copy = remote(
                    hid.at[:, columns(zz, wanted, j, yh, cc)],
                    held.at[slot, pl.ds(block * rows, rows)],
                    near_send.at[j * 2 + yh, n],
                    near_recv.at[slot, n % 2],
                    sharers[n],
                )
                near_copies.append(copy)
                if len(near_copies) <= EARLY:
                    copy.start()
    own, swaps = [], []
    for slot in range(8):
        j, kind, yh = slot // 4, slot // 2 % 2, slot % 2
        own.append(
            pltpu.make_async_copy(
                hid.at[:, columns(z, kind, j, yh, core)], held.at[slot, pl.ds(0, rows)], hid_own.at[slot]
            )
        )
        own[slot].start()
        copy = remote(
            hid.at[:, columns(z, kind, j, yh, 1 - core)],
            held.at[slot, pl.ds(rows, rows)],
            hid_send.at[slot],
            hid_recv.at[slot],
            pair,
        )
        copy.start()
        swaps.append(copy)

    places = [order[2 * ctx], order[2 * ctx + 1]]
    for qb in range(2):
        mask_bias(places[qb], lens, bias.at[qb])
    dvw[...] = jnp.zeros_like(dvw)
    dkw[...] = jnp.zeros_like(dkw)
    def all_here(which, src, dst):
        loads[which].wait()
        for o in FAR_FIRST:
            theirs = pl.ds(pl.multiple_of(lax.rem(ctx + 8 - o, 8) * rows, rows), rows)
            remote(src, dst.at[theirs], kv_send.at[which, o], kv_recv.at[which, o], ctx_peers[o - 1]).wait_recv()

    reach = pl.ds(0, WINDOW * SPAN)
    steps = 2 * 16 // GROUP
    scale = 1.0 / math.sqrt(HEAD)
    all_here(0, k_hbm, kall)
    loads[2].wait()
    for qb in range(2):
        window_of(order, places[qb], kall, k7.at[qb])

    def numerator_step(it, carry):
        qb, grp = it // (steps // 2), lax.rem(it, steps // 2)
        queries = heads_of(q_ref, qb, grp)[2]
        softmax_numerators(k7.at[qb], queries, bias.at[qb], expo_all.at[it], inv_all.at[it])
        return carry

    lax.fori_loop(0, steps, numerator_step, 0)
    all_here(1, v_hbm, vall)
    loads[3].wait()
    for qb in range(2):
        window_of(order, places[qb], vall, v7.at[qb])

    def score_step(it, carry):
        qb, grp = it // (steps // 2), lax.rem(it, steps // 2)
        cots = heads_of(g_ref, qb, grp)[2]
        softmax_terms(v7.at[qb], cots, expo_all.at[it], inv_all.at[it], d_scr, p_scr, ds_all.at[it])
        dvw[qb, reach, :] += jnp.dot(p_scr[...], cots, preferred_element_type=F32)
        return carry

    lax.fori_loop(0, steps, score_step, 0)

    def exchange(out, into, send, recv):
        copies = []
        for o in FAR_FIRST:
            copy = remote(out.at[lax.rem(ctx + o, 8)], into.at[o], send.at[o], recv.at[o], ctx_peers[o - 1])
            copy.start()
            copies.append(copy)
        return copies

    messages(order, places, dvw, dv_out, 1.0)
    dv_copies = exchange(dv_out, dv_in, dv_send, dv_recv)

    def key_step(it, carry):
        qb, grp = it // (steps // 2), lax.rem(it, steps // 2)
        queries = heads_of(q_ref, qb, grp)[2]
        dkw[qb, reach, :] += jnp.dot(ds_all[it], queries, preferred_element_type=F32)
        return carry

    lax.fori_loop(0, steps, key_step, 0)
    messages(order, places, dkw, dk_out, scale)
    dk_copies = exchange(dk_out, dk_in, dk_send, dk_recv)

    for qb in range(2):
        k7t[qb] = k7[qb].astype(F32).T.astype(BF16)

    def query_step(it, carry):
        qb, grp = it // (steps // 2), lax.rem(it, steps // 2)
        query_rows, lanes, _ = heads_of(q_ref, qb, grp)
        dq = (jnp.dot(k7t[qb], ds_all[it], preferred_element_type=F32) * scale).T.astype(BF16)
        for h in range(GROUP):
            dq_ref[query_rows, lanes[h]] = dq[h * SPAN : (h + 1) * SPAN, :]
        return carry

    lax.fori_loop(0, steps, query_step, 0)
    dq_copy = pltpu.make_async_copy(dq_ref, dq_hbm, load_sem.at[4])
    dq_copy.start()

    dkv_copies = []
    for side, (copies, out, into) in enumerate(((dk_copies, dk_out, dk_in), (dv_copies, dv_out, dv_in))[::-1]):
        for copy in copies:
            copy.wait()
        value = decode(out.at[ctx])
        for o in range(1, 8):
            value = value + decode(into.at[o])
        lanes = pl.ds((1 - side) * HEAD, HEAD)
        dkv2[pl.ds(0, rows), lanes] = value.astype(BF16)
        for n, device in enumerate([pair, *sharers]):
            start, arrival = rows, 0
            if n:
                arrival = 1 + 2 * wanted + (n - 1) % 2
                start = (1 + arrival) * rows
            copy = remote(
                dkv2.at[pl.ds(0, rows), lanes],
                dkv2.at[pl.ds(pl.multiple_of(start, rows), rows), lanes],
                pair_send.at[side, n],
                pair_recv.at[side, arrival],
                device,
            )
            copy.start()
            dkv_copies.append(copy)
    for copy in near_copies[EARLY:]:
        copy.start()
    for side in range(2):
        for n in range(5):
            lanes = pl.ds((1 - side) * HEAD, HEAD)
            remote(
                dkv2.at[pl.ds(0, rows), lanes],
                dkv2.at[pl.ds((1 + n) * rows, rows), lanes],
                pair_send.at[side, n],
                pair_recv.at[side, n],
                pair,
            ).wait_recv()
    dkvt[...] = dkv2[...].astype(F32).T.astype(BF16)

    rings = ((x_ring, y_ring), (y_ring, x_ring))
    pending = []

    def flat(value):
        return value.reshape(-1, 128)

    def piece(part, g, place, high):
        return flat(first[part, g, place, pl.ds(4 * high, 4)])

    def copy_of(part, g, k):
        device = rings[part][0][1 if k % 2 == 0 else 3]
        return remote(out1.at[part, g, k], in1.at[part, g, k], send1.at[part, g, k], recv1.at[part, g, k], device)

    def post(part, g, k, value):
        encode(value, out1.at[part, g, k])
        copy = copy_of(part, g, k)
        copy.start()
        pending.append(copy)

    def arrived(part, g, k):
        copy_of(part, g, k).wait_recv()
        return decode(in1.at[part, g, k])

    def begin(part, g):
        place = rings[part][0][0]
        after, before, opposite = lax.rem(place + 1, 4), lax.rem(place + 3, 4), lax.rem(place + 2, 4)
        for k, (owner, high) in enumerate(((opposite, 0), (opposite, 1), (after, 1), (before, 0))):
            post(part, g, k, piece(part, g, owner, high))

    def relay(part, g):
        place = rings[part][0][0]
        after, before = lax.rem(place + 1, 4), lax.rem(place + 3, 4)
        for k, (owner, high) in enumerate(((after, 0), (before, 1))):
            post(part, g, 4 + k, arrived(part, g, k) + piece(part, g, owner, high))

    def finish(part, g):
        place = rings[part][0][0]
        low = arrived(part, g, 3) + arrived(part, g, 4) + piece(part, g, place, 0)
        high = arrived(part, g, 2) + arrived(part, g, 5) + piece(part, g, place, 1)
        return low, high

    def direct(part, g, k):
        return remote(
            out2.at[part, g, k], in2.at[part, g, k], send2.at[part, g, k], recv2.at[part, g, k], rings[part][1][k]
        )

    def compute(g):
        for slot in range(4 * g, 4 * g + 4):
            own[slot].wait()
            swaps[slot].wait()
            for c in range(2):
                block = pl.ds((2 + c) * rows, rows)
                remote(
                    hid.at[:, pl.ds(0, 512)], held.at[slot, block], near_send.at[0, 0], near_recv.at[slot, c], pair
                ).wait_recv()

        def block(k, carry):
            kind, yh = k // 2, lax.rem(k, 2)
            theirs = pl.ds(pl.multiple_of(2 * rows * (1 + kind), 128), 2 * rows)
            here, both = pl.ds(0, 2 * rows), pl.ds(2 * rows, 2 * rows)
            product = jnp.dot(dkvt[:, 0 : 2 * rows], held[4 * g + k, here], preferred_element_type=F32)
            product = product + jnp.dot(
                dkvt[:, theirs], held[4 * g + k, both], preferred_element_type=F32
            )
            for xx in range(4):
                for yl in range(2):
                    r0 = (xx * 2 + yl) * 32
                    yy = yh * 2 + yl
                    for side in range(2):
                        first[0, g, xx, yy * 2 + kind, side] = product[r0 : r0 + 32, side * 128 : side * 128 + 128]
                        first[1, g, yy, xx * 2 + kind, side] = product[r0 : r0 + 32, side * 128 + 256 : side * 128 + 384]
            return carry

        lax.fori_loop(0, 4, block, 0)
        for part in range(2):
            begin(part, g)

    def middle(g):
        for part in range(2):
            low, high = finish(part, g)
            for t in range(4):
                half = (low, high)[t // 2].reshape(2, 2, 2, 32, 128)
                second[part, g, t] = half[t % 2]
            place = rings[part][1][0]
            for k in (2, 1, 3):
                encode(flat(second[part, g, lax.rem(place + k, 4)]), out2.at[part, g, k])
                copy = direct(part, g, k)
                copy.start()
                pending.append(copy)

    def last(g):
        parts = []
        for part in range(2):
            value = flat(second[part, g, rings[part][1][0]])
            for k in (1, 3, 2):
                direct(part, g, k).wait_recv()
                value = value + decode(in2.at[part, g, k])
            parts.append(value.reshape(2, 64, 128))
        for kind in range(2):
            slot = 2 * g + kind
            value = jnp.concatenate([parts[0][kind], parts[1][kind]], axis=0)
            o = DISTANCES[g][kind]
            if o == 0:
                total[...] = value
                continue
            encode(value, z_out.at[slot])
            copy = remote(z_out.at[slot], z_in.at[o], z_send.at[o], z_recv.at[o], even_peers[o // 2 - 1])
            copy.start()
            pending.append(copy)

    compute(0)
    for part in range(2):
        relay(part, 0)
    compute(1)
    middle(0)
    for part in range(2):
        relay(part, 1)
    last(0)
    middle(1)
    last(1)

    sums = total[...]
    for o in (4, 2, 6):
        remote(z_out.at[0], z_in.at[o], z_send.at[o], z_recv.at[o], even_peers[o // 2 - 1]).wait_recv()
        sums = sums + decode(z_in.at[o])
    encode(sums, ag_out)
    copies = []
    for o in FAR_FIRST:
        copy = remote(ag_out, ag_in.at[o], ag_send.at[o], ag_recv.at[o], ctx_peers[o - 1])
        copy.start()
        copies.append(copy)
    out_ref[ctx] = decode(ag_out).reshape(4, 32, 128)
    for copy in pending:
        copy.wait_send()
    for copy in [*kv_copies, *near_copies, *dkv_copies]:
        copy.wait_send()
    dq_copy.wait()
    for copy in copies:
        copy.wait()
    for o in range(1, 8):
        out_ref[lax.rem(ctx + 8 - o, 8)] = decode(ag_in.at[o]).reshape(4, 32, 128)


def backward(order, lens, queries, cots, keys, values, hidden):
    rows = hidden.shape[0]
    dma = pltpu.SemaphoreType.DMA
    codes = jnp.int16
    reach, width = WINDOW * SPAN, GROUP * SPAN
    hbm = pl.BlockSpec(memory_space=pl.ANY)
    smem = pl.BlockSpec(memory_space=pltpu.SMEM)
    return pl.pallas_call(
        backward_kernel,
        out_shape=[
            jax.ShapeDtypeStruct(queries.shape, BF16),
            jax.ShapeDtypeStruct((8, 4, 32, 128), F32),
        ],
        in_specs=[smem, smem, hbm, hbm, hbm, hbm, hbm],
        out_specs=[hbm, pl.BlockSpec(memory_space=pltpu.VMEM)],
        scratch_shapes=[
            pltpu.VMEM(queries.shape, BF16),
            pltpu.VMEM(queries.shape, BF16),
            pltpu.VMEM((8 * rows, HEAD), BF16),
            pltpu.VMEM((8 * rows, HEAD), BF16),
            pltpu.VMEM((2, reach, HEAD), BF16),
            pltpu.VMEM((2, reach, HEAD), BF16),
            pltpu.VMEM((2, HEAD, reach), BF16),
            pltpu.VMEM((2, reach, width), F32),
            pltpu.VMEM((32 // GROUP, reach, width), F32),
            pltpu.VMEM((32 // GROUP, 8, width), F32),
            pltpu.VMEM((reach, width), F32),
            pltpu.VMEM((reach, width), BF16),
            pltpu.VMEM((32 // GROUP, reach, width), BF16),
            pltpu.VMEM((2, reach, HEAD), F32),
            pltpu.VMEM((2, reach, HEAD), F32),
            pltpu.VMEM((8, rows + 16, HEAD), codes),
            pltpu.VMEM((8, rows + 16, HEAD), codes),
            pltpu.VMEM((8, rows + 16, HEAD), codes),
            pltpu.VMEM((8, rows + 16, HEAD), codes),
            pltpu.VMEM(queries.shape, BF16),
            dma((5,)), dma((2, 8)), dma((2, 8)), dma((8,)), dma((8,)), dma((8,)), dma((8,)),
            pltpu.VMEM((8, 4 * rows, 512), BF16),
            pltpu.VMEM((6 * rows, 256), BF16),
            pltpu.VMEM((256, 6 * rows), BF16),
            pltpu.VMEM((2, NGROUPS, 4, 8, 2, 32, 128), F32),
            pltpu.VMEM((2, NGROUPS, 6, 272, 128), codes),
            pltpu.VMEM((2, NGROUPS, 6, 272, 128), codes),
            pltpu.VMEM((2, NGROUPS, 4, 2, 2, 32, 128), F32),
            pltpu.VMEM((2, NGROUPS, 4, 144, 128), codes),
            pltpu.VMEM((2, NGROUPS, 4, 144, 128), codes),
            pltpu.VMEM((8, 144, 128), codes),
            pltpu.VMEM((8, 144, 128), codes),
            pltpu.VMEM((128, 128), F32),
            pltpu.VMEM((144, 128), codes),
            pltpu.VMEM((8, 144, 128), codes),
            dma((8,)), dma((8,)), dma((8,)), dma((4, 4)), dma((8, 2)), dma((2, 5)), dma((2, 5)),
            dma((2, NGROUPS, 6)), dma((2, NGROUPS, 6)), dma((2, NGROUPS, 4)), dma((2, NGROUPS, 4)),
            dma((8,)), dma((8,)), dma((8,)), dma((8,)),
        ],
        compiler_params=pltpu.CompilerParams(
            collective_id=0, has_side_effects=True, vmem_limit_bytes=60 * 2**20
        ),
        name="backward",
    )(order, lens, queries, cots, keys, values, hidden)


def adam_kernel(
    dq_in, grad_t, m_codes, m_scales, v_codes, v_scales, dq, update, m_norm, m_absmax, v_norm, v_absmax, grad
):
    dq[...] = dq_in[...]
    for half in range(2):
        grad[pl.ds(half * 128, 128), :] = grad_t[:, half].reshape(256, 128).T
    base = pl.program_id(0) * 32
    for b in range(32):
        rows = pl.ds(b * 8, 8)
        g = grad[rows, :]
        m = 0.9 * (m_codes[rows, :].astype(F32) * (m_scales[base + b] * (1.0 / 127.0))) + 0.1 * g
        v = 0.95 * (v_codes[rows, :].astype(F32) * (v_scales[base + b] * (1.0 / 255.0))) + 0.05 * g * g
        update[rows, :] = m * (1.0 / (1.0 - 0.9**STEP)) / (jnp.sqrt(v * (1.0 / (1.0 - 0.95**STEP))) + 1e-08)
        m_top = jnp.max(jnp.abs(m))
        v_top = jnp.max(v)
        m_absmax[base + b] = m_top
        v_absmax[base + b] = v_top
        m_norm[rows, :] = m / (m_top + 1e-06)
        v_norm[rows, :] = v / (v_top + 1e-06)


def adam(dq, grad_t, m_codes, m_scales, v_codes, v_scales):
    smem = pl.BlockSpec(memory_space=pltpu.SMEM)
    rows = pl.BlockSpec((256, 256), lambda q: (q, 0))
    slab = pl.BlockSpec((dq.shape[0] // 2, dq.shape[1]), lambda q: (q, 0))
    big = jax.ShapeDtypeStruct(m_codes.shape, F32)
    small = jax.ShapeDtypeStruct(m_scales.shape, F32)
    return pl.pallas_call(
        adam_kernel,
        grid=(2,),
        out_shape=[jax.ShapeDtypeStruct(dq.shape, dq.dtype), big, big, small, big, small],
        in_specs=[slab, pl.BlockSpec((8, 2, 32, 128), lambda q: (0, q, 0, 0)), rows, smem, rows, smem],
        out_specs=[slab, rows, rows, smem, rows, smem],
        scratch_shapes=[pltpu.VMEM((256, 256), F32)],
        compiler_params=pltpu.CompilerParams(vmem_limit_bytes=60 * 2**20),
        name="adam",
    )(dq, grad_t, m_codes, m_scales, v_codes, v_scales)


def shards(
    q_heads, keys, values, out_grad, hidden_in, doc_lengths, span_order, m_codes, m_scales, v_codes, v_scales
):
    dq, grad_t = backward(
        span_order, doc_lengths, q_heads[0], out_grad[0], keys[0], values[0], hidden_in[0]
    )
    dq, update, m_norm, m_absmax, v_norm, v_absmax = adam(dq, grad_t, m_codes, m_scales, v_codes, v_scales)
    return (dq[None], update, m_norm, m_absmax, v_norm, v_absmax)


def solution(mesh):
    in_specs = (
        P("dp", "ctx", None),
        P("dp", "ctx", None),
        P("dp", "ctx", None),
        P("dp", "ctx", None),
        P("dp", "ctx", None),
        P("dp", None),
        P(),
        P("dp", None),
        P("dp"),
        P("dp", None),
        P("dp"),
    )
    out_specs = (
        P("dp", "ctx", None),
        P("dp", None),
        P("dp", None),
        P("dp"),
        P("dp", None),
        P("dp"),
    )
    return jax.shard_map(shards, mesh=mesh, in_specs=in_specs, out_specs=out_specs, check_vma=False)
```
